32 devices in a mesh: doc: 2 (over x), seq: 16 (over z, y, core).
Axes of the slice: x: 2, y: 2, z: 4, core: 2. Of those that a mesh axis runs over, the one named last changes fastest.
Arguments:
- queries: bfloat16 [2, 2048, 1024], P('doc', 'seq'), may hold values from -7 to 7
- key_rows: bfloat16 [2, 2048, 1024], P('doc', 'seq'), may hold values from -7 to 7
- value_rows: bfloat16 [2, 2048, 1024], P('doc', 'seq'), may hold values from -5 to 5
- cotangent: bfloat16 [2, 2048, 1024], P('doc', 'seq'), may hold values from -3 to 3
- out_weight: bfloat16 [1024, 1024], P('doc'), may hold values from -0.1875 to 0.1875
- lengths: int32 [2, 4], P('doc'), may hold values from 1 to 16, 32 in all within a row
- upweight: int32 [2, 4], P('doc'), may hold values from 1 to 6, as said below
Outputs:
- layer_out: bfloat16 [2, 2048, 1024], P('doc', 'seq')
- grad_query: bfloat16 [2, 2048, 1024], P('doc', 'seq')
- grad_key: bfloat16 [2, 2048, 1024], P('doc', 'seq')
- grad_value: bfloat16 [2, 2048, 1024], P('doc', 'seq')
- grad_weight: float32 [1024, 1024], P('doc')
The draws below stay inside these ranges and needn't reach their ends.
Inputs may be any that keep to these rules, and one draw needn't show every extreme that they name: Each sequence's documents fill it exactly: the lengths add up to 32, and the longest is 16. `upweight`: each entry is 1 or 6; every sequence has a document with factor 6.
All inputs are finite; a program needn't handle non-finite values.
Results may differ from the reference program's by a relative error of at most 0.0089.
Values may be sent and summed in bfloat16 or wider, within the bound.
No kernel may reach another device: no remote copies, remote signals or barrier semaphores. Data moves between devices by JAX's collectives and lax.ppermute only.
A program may use at most 128 MiB of HBM per device.

```python
import math
import jax
import jax.numpy as jnp
import numpy as np
from jax import lax

HEADS = 16
HEAD_DIM = 64
D = 1024
WINDOW = 512
TOK_DEV = 128
BLOCK = 64
DOCS = 4
LAMBDA = 6
SEQS = 2
SEQ_LEN = 2048
MOST_BLOCKS = 16


def paired_draw(key):
    paired_seed = jax.random.fold_in(key, 9173)
    query_seed, key_seed = jax.random.split(paired_seed, 2)
    full_shape = (SEQS, SEQ_LEN, HEADS * HEAD_DIM)
    query_draw = jnp.clip(jax.random.normal(query_seed, full_shape, jnp.float32), -3.5, 3.5) * 1.6
    key_draw = jnp.clip(jax.random.normal(key_seed, full_shape, jnp.float32), -3.5, 3.5) * 1.6
    return (query_draw, key_draw)


def draw_queries(key, part):
    return paired_draw(key)[0].astype(jnp.bfloat16)


def draw_key_rows(key, part):
    return paired_draw(key)[1].astype(jnp.bfloat16)


def draw_upweight(key, part):
    pick_seed, forced_seed = jax.random.split(jax.random.fold_in(key, 4242))
    chosen = jax.random.randint(pick_seed, (SEQS, DOCS), 0, 3)
    forced_doc = jax.random.randint(forced_seed, (SEQS, 1), 0, DOCS)
    marked = (chosen == 0) | (jnp.arange(DOCS)[None, :] == forced_doc)
    return jnp.where(marked, LAMBDA, 1).astype(jnp.int32)


def level_of(own_key, extent, cuts, low, largest):
    factor_of = 1.0
    for position, shards_of in cuts:
        steps = jax.random.uniform(jax.random.fold_in(jax.random.fold_in(own_key, 6), position), (shards_of,), jnp.float32, low / len(cuts), largest / len(cuts))
        factor_of = factor_of * jnp.repeat(jnp.exp(steps), extent[position] // shards_of).reshape((-1,) + (1,) * (len(extent) - 1 - position))
    return factor_of


def length_profile(count, total, bound, skew):
    portions = [(1 << 20) // math.isqrt(grade ** skew) + 1 for grade in range(2, count + 1)]
    surplus, holding = total - bound - (count - 1), [1] * (count - 1)
    while surplus > 0:
        movable = [i for i in range(count - 1) if holding[i] < bound]
        pool, budget = sum([portions[i] for i in movable]), surplus
        for i in movable:
            more = min(bound - holding[i], max(1, budget * portions[i] // pool), surplus)
            holding[i] = holding[i] + more
            surplus = surplus - more
    return np.array([bound] + holding)


def uneven(stream_key, amount, total, limit, skew):
    if amount == 2:
        one = jax.random.randint(stream_key, (), max(1, total - limit), min(limit, total - 1) + 1)
        return jnp.stack([one, total - one])
    tallies = jnp.asarray(length_profile(amount, total, limit, skew), jnp.int32)
    twos = (amount - 1) // 2
    source_of, taker = tallies[1:1 + 2 * twos:2], tallies[2:2 + 2 * twos:2]
    room = jnp.minimum(source_of - 1, limit - taker)
    moved = jax.random.randint(jax.random.fold_in(stream_key, 1), (twos,), 0, 1 << 20) % (room + 1)
    tallies = tallies.at[1:1 + 2 * twos:2].set(source_of - moved).at[2:2 + 2 * twos:2].set(taker + moved)
    return tallies[jax.random.permutation(jax.random.fold_in(stream_key, 2), amount)]


def bell_draw(key, dims, scale, bound, pieces=(), kind=jnp.bfloat16):
    result = jax.random.normal(key, dims, jnp.float32) * scale
    if len(pieces) > 0:
        result = level_of(key, dims, pieces, -0.22, 0.18) * result
    return jnp.clip(result, min=-bound, max=bound).astype(kind)


def setup_inputs(seed: int = 0) -> dict:
    splits = jax.random.split(jax.random.key(seed), 8)
    return {
        "queries": draw_queries(jax.random.fold_in(splits[7], 71), 0),
        "key_rows": draw_key_rows(jax.random.fold_in(splits[7], 71), 0),
        "value_rows": bell_draw(splits[2], (SEQS, SEQ_LEN, D), 1.0, 5.0, ((0, 2), (1, 16))),
        "cotangent": bell_draw(splits[3], (SEQS, SEQ_LEN, D), 0.5, 3.0, ((0, 2), (1, 16))),
        "out_weight": bell_draw(splits[4], (D, D), D ** -0.5, 0.1875, ((0, 2),)),
        "lengths": jax.vmap(lambda own: uneven(own, DOCS, SEQ_LEN // BLOCK, MOST_BLOCKS, 2))(jax.random.split(splits[5], SEQS)).reshape((SEQS, DOCS)).astype(jnp.int32),
        "upweight": draw_upweight(jax.random.fold_in(splits[7], 71), 0),
    }


def document_ids(lengths_row, positions):
    bounds = (jnp.cumsum(lengths_row) * BLOCK).astype(jnp.int32)
    return lax.optimization_barrier(jnp.sum((positions[:, None] >= bounds[None, :]).astype(jnp.int32), axis=1)).astype(jnp.int32)

def band_mask(query_pos, key_pos, query_doc, key_doc, seq_len):
    near_band = jnp.abs(query_pos[:, None] - key_pos[None, :]) <= WINDOW
    inside = (key_pos >= 0) & (key_pos < seq_len)
    return near_band & inside[None, :] & (query_doc[:, None] == key_doc[None, :])

def soft_weights(query_blk, key_blk, allowed):
    scores = jnp.einsum('qhd,khd->hqk', query_blk.astype(jnp.float32), key_blk.astype(jnp.float32)) * HEAD_DIM ** (-0.5)
    scores = jnp.where(allowed[None], scores, -jnp.inf)
    row_peak = lax.optimization_barrier(jnp.max(scores, axis=2, keepdims=True))
    exponent = jnp.exp(scores - row_peak)
    return exponent / lax.optimization_barrier(jnp.sum(exponent, axis=2, keepdims=True))

def settle(values):
    return lax.optimization_barrier(values.astype(jnp.bfloat16)).astype(jnp.float32)

def reference(queries, key_rows, value_rows, cotangent, out_weight, lengths, upweight):
    model_width = HEADS * HEAD_DIM
    key_span = TOK_DEV + 2 * WINDOW
    block_count = SEQ_LEN // TOK_DEV
    score_scale = HEAD_DIM ** (-0.5)
    offsets = jnp.arange(TOK_DEV, dtype=jnp.int32)
    key_offsets = jnp.arange(key_span, dtype=jnp.int32)
    foreign = (key_offsets < WINDOW) | (key_offsets >= WINDOW + TOK_DEV)

    def sequence_pass(sequence_items):
        seq_query, seq_key, seq_value, seq_cot, lengths_row, upweight_row = sequence_items
        key_pad = jnp.pad(seq_key, ((WINDOW, WINDOW), (0, 0)))
        value_pad = jnp.pad(seq_value, ((WINDOW, WINDOW), (0, 0)))
        positions = jnp.arange(SEQ_LEN, dtype=jnp.int32)
        token_doc = document_ids(lengths_row, positions)
        matches = token_doc[:, None] == jnp.arange(DOCS, dtype=jnp.int32)[None, :]
        token_weight = lax.optimization_barrier(jnp.sum(jnp.where(matches, upweight_row[None, :], 0), axis=1)).astype(jnp.float32)

        def block_pieces(block_index):
            row_start = (block_index * TOK_DEV).astype(jnp.int32)
            query_blk = lax.dynamic_slice_in_dim(seq_query, row_start, TOK_DEV, 0).reshape(TOK_DEV, HEADS, HEAD_DIM)
            key_blk = lax.dynamic_slice_in_dim(key_pad, row_start, key_span, 0).reshape(key_span, HEADS, HEAD_DIM)
            value_blk = lax.dynamic_slice_in_dim(value_pad, row_start, key_span, 0).reshape(key_span, HEADS, HEAD_DIM)
            query_pos = row_start + offsets
            key_pos = row_start - WINDOW + key_offsets
            allowed = band_mask(query_pos, key_pos, document_ids(lengths_row, query_pos), document_ids(lengths_row, key_pos), SEQ_LEN)
            return (row_start, query_blk, key_blk, value_blk, allowed)

        def forward_block(block_index):
            row_start, query_blk, key_blk, value_blk, allowed = block_pieces(block_index)
            prob_half = soft_weights(query_blk, key_blk, allowed).astype(jnp.bfloat16)
            mixed_rows = jnp.einsum('hqk,khd->qhd', prob_half.astype(jnp.float32), value_blk.astype(jnp.float32))
            return mixed_rows.reshape(TOK_DEV, model_width).astype(jnp.bfloat16)
        attended = lax.map(forward_block, jnp.arange(block_count, dtype=jnp.int32)).reshape(SEQ_LEN, model_width)
        layer_out = jnp.dot(attended, out_weight, preferred_element_type=jnp.float32).astype(jnp.bfloat16)
        grad_out = (token_weight[:, None] * seq_cot.astype(jnp.float32)).astype(jnp.bfloat16)
        weight_part = jnp.dot(attended.T, grad_out, preferred_element_type=jnp.float32)
        grad_attended = jnp.dot(grad_out, out_weight.T, preferred_element_type=jnp.float32).astype(jnp.bfloat16)

        def backward_block(grad_sums, block_index):
            key_sum, value_sum = grad_sums
            row_start, query_blk, key_blk, value_blk, allowed = block_pieces(block_index)
            prob_full = soft_weights(query_blk, key_blk, allowed)
            prob_half = prob_full.astype(jnp.bfloat16)
            grad_blk = lax.dynamic_slice_in_dim(grad_attended, row_start, TOK_DEV, 0).reshape(TOK_DEV, HEADS, HEAD_DIM)
            grad_prob = jnp.einsum('qhd,khd->hqk', grad_blk.astype(jnp.float32), value_blk.astype(jnp.float32))
            centre = lax.optimization_barrier(jnp.sum(prob_full * grad_prob, axis=2, keepdims=True))
            grad_score = (prob_full * (grad_prob - centre) * score_scale).astype(jnp.bfloat16)
            grad_query_blk = jnp.einsum('hqk,khd->qhd', grad_score.astype(jnp.float32), key_blk.astype(jnp.float32))
            grad_query_blk = grad_query_blk.reshape(TOK_DEV, model_width).astype(jnp.bfloat16)
            key_part = jnp.einsum('hqk,qhd->khd', grad_score.astype(jnp.float32), query_blk.astype(jnp.float32))
            value_part = jnp.einsum('hqk,qhd->khd', prob_half.astype(jnp.float32), grad_blk.astype(jnp.float32))
            key_part = key_part.reshape(key_span, model_width)
            value_part = value_part.reshape(key_span, model_width)
            key_part = jnp.where(foreign[:, None], settle(key_part), key_part)
            value_part = jnp.where(foreign[:, None], settle(value_part), value_part)
            key_sum = lax.dynamic_update_slice_in_dim(key_sum, lax.dynamic_slice_in_dim(key_sum, row_start, key_span, 0) + key_part, row_start, 0)
            value_sum = lax.dynamic_update_slice_in_dim(value_sum, lax.dynamic_slice_in_dim(value_sum, row_start, key_span, 0) + value_part, row_start, 0)
            return ((key_sum, value_sum), grad_query_blk)
        zero_pad = jnp.zeros((SEQ_LEN + 2 * WINDOW, model_width), jnp.float32)
        (key_sum, value_sum), grad_query = lax.scan(backward_block, (zero_pad, zero_pad), jnp.arange(block_count, dtype=jnp.int32))
        grad_key = key_sum[WINDOW:WINDOW + SEQ_LEN].astype(jnp.bfloat16)
        grad_value = value_sum[WINDOW:WINDOW + SEQ_LEN].astype(jnp.bfloat16)
        return (layer_out, grad_query.reshape(SEQ_LEN, model_width), grad_key, grad_value, weight_part)
    results = lax.map(sequence_pass, (queries, key_rows, value_rows, cotangent, lengths, upweight))
    layer_out, grad_query, grad_key, grad_value, weight_parts = results
    grad_weight = lax.optimization_barrier(jnp.sum(weight_parts, axis=0)) * (1.0 / math.sqrt(SEQS * SEQ_LEN))
    return (layer_out, grad_query, grad_key, grad_value, grad_weight)
```

```python
import functools
import math

import jax
import jax.numpy as jnp
from jax import lax
from jax.experimental import pallas as pl
from jax.experimental.pallas import tpu as pltpu
from jax.sharding import PartitionSpec as P

HEADS = 16
HEAD_DIM = 64
WINDOW = 512
BLOCK = 64
DOCS = 4
PAIR = 2 * HEAD_DIM
MASKED = -1e30
BF16 = jnp.bfloat16
F32 = jnp.float32

VMEM = pl.BlockSpec(memory_space=pltpu.VMEM)
SMEM = pl.BlockSpec(memory_space=pltpu.SMEM)


def call(kernel, out_shape, operands, scalars=0, scratch=(), flops=0, moved=0, vmem=24):
    outs = [jax.ShapeDtypeStruct(shape, kind) for shape, kind in out_shape]
    return pl.pallas_call(
        kernel,
        out_shape=outs,
        in_specs=[SMEM] * scalars + [VMEM] * (len(operands) - scalars),
        out_specs=[VMEM] * len(outs),
        scratch_shapes=list(scratch),
        compiler_params=pltpu.CompilerParams(vmem_limit_bytes=vmem << 20),
        cost_estimate=pl.CostEstimate(flops=flops, bytes_accessed=moved, transcendentals=0),
    )(*operands)


def dot_nn(a, b):
    return lax.dot_general(a, b, (((1,), (0,)), ((), ())), preferred_element_type=F32)


def dot_nt(a, b):
    return lax.dot_general(a, b, (((1,), (1,)), ((), ())), preferred_element_type=F32)


def doc_bounds(len_ref):
    ends = []
    total = 0
    for d in range(DOCS):
        total = total + len_ref[0, d] * BLOCK
        ends.append(total)
    return ends


def pack_kernel(group, len_ref, up_ref, q_ref, k_ref, v_ref, cot_ref, *outs):
    kv, qs, weighted = outs[:group], outs[group : 2 * group], outs[2 * group]
    rows = q_ref.shape[0]
    cols = q_ref.shape[1] // group
    place = lax.axis_index("seq")
    inner = lax.rem(place, group)
    for m in range(group):
        start = pl.multiple_of((inner ^ m) * cols, 128)
        kv[m][0:rows, :] = k_ref[:, pl.ds(start, cols)]
        kv[m][rows : 2 * rows, :] = v_ref[:, pl.ds(start, cols)]
        qs[m][...] = q_ref[:, pl.ds(start, cols)]
    ends = doc_bounds(len_ref)
    pos = place * rows + lax.broadcasted_iota(jnp.int32, (rows, 1), 0)
    factor = jnp.full((rows, 1), up_ref[0, 0], jnp.int32)
    for d in range(1, DOCS):
        factor = jnp.where(pos >= ends[d - 1], up_ref[0, d], factor)
    weighted[...] = (factor.astype(F32) * cot_ref[...].astype(F32)).astype(BF16)


def key_bias(len_ref, plane_start, block, rows, span):
    ends = doc_bounds(len_ref)
    first = plane_start + block * rows
    query = first + lax.broadcasted_iota(jnp.int32, (1, rows), 1)
    low = jnp.zeros((1, rows), jnp.int32)
    high = jnp.full((1, rows), ends[DOCS - 1], jnp.int32)
    for d in range(DOCS - 1):
        low = jnp.where(query >= ends[d], ends[d], low)
        high = jnp.where(query < ends[DOCS - 2 - d], ends[DOCS - 2 - d], high)
    low = jnp.maximum(low, query - WINDOW)
    high = jnp.minimum(high, query + WINDOW + 1)
    key = first - WINDOW + lax.broadcasted_iota(jnp.int32, (span, rows), 0)
    bias = jnp.where((key >= low) & (key < high), 0.0, MASKED).astype(F32)
    return jnp.concatenate([bias, bias], axis=1)


def stack_pair(block):
    lane = lax.broadcasted_iota(jnp.int32, block.shape, 1)
    zero = jnp.zeros_like(block)
    return jnp.concatenate(
        [jnp.where(lane < HEAD_DIM, block, zero), jnp.where(lane < HEAD_DIM, zero, block)], axis=0
    )


def unstack_pair(both, rows):
    return jnp.concatenate([both[:HEAD_DIM, :rows], both[HEAD_DIM:, rows:]], axis=0)


LOG2_SCALE = math.log2(math.e) * HEAD_DIM ** (-0.5)


def forward_kernel(group, len_ref, *refs):
    q_in, own, before, after = (refs[group * i : group * (i + 1)] for i in range(4))
    keys, vals, keys_t, queries, att_t, stats = refs[4 * group : 4 * group + 6]
    pieces = refs[4 * group + 6 : 5 * group + 6]
    vals_t, att = refs[5 * group + 6 :]
    rows, cols = q_in[0].shape
    plane = group * rows
    span = rows + 2 * WINDOW
    place = lax.axis_index("seq")
    inner = lax.rem(place, group)
    plane_start = (place - inner) * rows
    for m in range(group):
        spot = (inner ^ m) * rows
        queries[pl.ds(pl.multiple_of(spot, 128), rows), :] = q_in[m][...]
        for side, source in enumerate((before, own, after)):
            at = pl.ds(pl.multiple_of(side * plane + spot, 128), rows)
            keys[at, :] = source[m][0:rows, :]
            vals[at, :] = source[m][rows : 2 * rows, :]
    keys_t[...] = keys[...].T
    vals_t[...] = vals[...].T
    for block in range(group):
        bias = key_bias(len_ref, plane_start, block, rows, span)
        at = slice(block * rows, (block + 1) * rows)
        seen = slice(block * rows, block * rows + span)
        for pair in range(cols // PAIR):
            lanes = slice(pair * PAIR, (pair + 1) * PAIR)
            score = dot_nt(keys[seen, lanes], stack_pair(queries[at, lanes])) + bias
            peak = jnp.max(score, axis=0, keepdims=True)
            power = jnp.exp2((score - peak) * LOG2_SCALE)
            share = 1.0 / jnp.sum(power, axis=0, keepdims=True)
            unit = block * (cols // PAIR) + pair
            stats[unit, 0:1, :] = peak
            stats[unit, 1:2, :] = share
            prob = (power * share).astype(BF16)
            mixed = unstack_pair(dot_nn(vals_t[lanes, seen], prob), rows).astype(BF16)
            att_t[lanes, at] = mixed
            att[at, lanes] = mixed.T
    for m in range(group):
        pieces[m][...] = att[pl.ds(pl.multiple_of((inner ^ m) * rows, 128), rows), :]


def middle_kernel(group, fast, len_ref, att_t, near, far, *refs):
    grads = refs[:group]
    grad_att = refs[group]
    out = refs[group + 1 : -3]
    grad_all, weight, total = refs[-3:]
    rows = grads[0].shape[0]
    cols = att_t.shape[0]
    half = near.shape[0] // cols
    place = lax.axis_index("seq")
    inner = lax.rem(place, group)
    first = lax.axis_index("doc") if fast else 0
    start = pl.multiple_of(lax.rem(inner, half) * cols, 128)

    @pl.when(inner // half == first)
    def _():
        weight[...] = near[pl.ds(start, cols), :]

    @pl.when(inner // half != first)
    def _():
        weight[...] = far[pl.ds(start, cols), :]

    for m in range(group):
        grad_all[pl.ds(pl.multiple_of((inner ^ m) * rows, 128), rows), :] = grads[m][...]
    product = dot_nn(att_t[...], grad_all[...])
    if fast:
        total[...] = product.astype(BF16)
        count = len(out)
        part = cols // count
        outer = place // group
        for m in range(count):
            out[m][...] = total[pl.ds(pl.multiple_of((outer ^ m) * part, 16), part), :]
    else:
        out[0][...] = product
    grad_att[...] = dot_nt(grad_all[...], weight[...]).astype(BF16)


def project_kernel(group, fast, near, far, *refs):
    pieces, out, att = refs[:group], refs[group], refs[group + 1]
    cols = pieces[0].shape[1]
    depth = near.shape[0]
    inner = lax.rem(lax.axis_index("seq"), group)
    first = lax.axis_index("doc") if fast else 0
    for m in range(group):
        att[:, pl.ds(pl.multiple_of((inner ^ m) * cols, 128), cols)] = pieces[m][...]
    left = att[:, pl.ds(pl.multiple_of(first * depth, 128), depth)]
    right = att[:, pl.ds(pl.multiple_of((1 - first) * depth, 128), depth)]
    out[...] = (dot_nn(left, near[...]) + dot_nn(right, far[...])).astype(BF16)


def backward_kernel(
    group, pair, pairs, len_ref, keys, vals, keys_t, queries, grad_att, stats,
    to_before, own, to_after, grad_query, key_sum, value_sum,
):
    plane = queries.shape[0]
    rows = plane // group
    span = rows + 2 * WINDOW
    place = lax.axis_index("seq")
    plane_start = (place - lax.rem(place, group)) * rows
    lanes = slice(pair * PAIR, (pair + 1) * PAIR)
    key_sum[...] = jnp.zeros_like(key_sum)
    value_sum[...] = jnp.zeros_like(value_sum)
    for block in range(group):
        bias = key_bias(len_ref, plane_start, block, rows, span)
        at = slice(block * rows, (block + 1) * rows)
        seen = slice(block * rows, block * rows + span)
        unit = block * pairs + pair
        query = stack_pair(queries[at, lanes])
        grad = stack_pair(grad_att[at, lanes])
        score = dot_nt(keys[seen, lanes], query) + bias
        prob = jnp.exp2((score - stats[unit, 0:1, :]) * LOG2_SCALE) * stats[unit, 1:2, :]
        grad_prob = dot_nt(vals[seen, lanes], grad)
        centre = jnp.sum(prob * grad_prob, axis=0, keepdims=True)
        grad_score = (prob * (grad_prob - centre) * HEAD_DIM ** (-0.5)).astype(BF16)
        value_sum[seen, :] += dot_nn(prob.astype(BF16), grad)
        key_sum[seen, :] += dot_nn(grad_score, query)
        turned = unstack_pair(dot_nn(keys_t[lanes, seen], grad_score), rows)
        grad_query[at, :] = turned.astype(BF16).T
    for target, kept in ((to_before, 0), (own, plane), (to_after, 2 * plane)):
        target[0:plane, :] = key_sum[kept : kept + plane, :].astype(target.dtype)
        target[plane : 2 * plane, :] = value_sum[kept : kept + plane, :].astype(target.dtype)


def settle_kernel(group, own, from_after, from_before, grad_query, *pieces):
    plane = grad_query.shape[0]
    rows = plane // group
    inner = lax.rem(lax.axis_index("seq"), group)
    for m in range(group):
        spot = (inner ^ m) * rows
        pieces[m][0:rows, :] = grad_query[pl.ds(pl.multiple_of(spot, 128), rows), :]
        for part in range(2):
            at = pl.ds(pl.multiple_of(part * plane + spot, 128), rows)
            summed = own[at, :] + from_after[at, :].astype(F32) + from_before[at, :].astype(F32)
            pieces[m][(part + 1) * rows : (part + 2) * rows, :] = summed.astype(BF16)


def unpack_kernel(group, *refs):
    outs = refs[-3:]
    pieces = refs[:-3]
    pairs = len(pieces) // group
    rows = outs[0].shape[0]
    cols = outs[0].shape[1] // group
    inner = lax.rem(lax.axis_index("seq"), group)
    for pair in range(pairs):
        for m in range(group):
            at = pl.ds(pl.multiple_of((inner ^ m) * cols + pair * PAIR, 128), PAIR)
            for part in range(3):
                outs[part][:, at] = pieces[pair * group + m][part * rows : (part + 1) * rows, :]


def finish_kernel(group, count, scale, *refs):
    out = refs[-1]
    near, far = refs[:count], refs[count : 2 * count]
    place = lax.axis_index("seq")
    side = lax.rem(place, 2)
    outer = place // group
    part = near[0].shape[0]
    for source, base in ((near, side), (far, 1 - side)):
        for m in range(count):
            start = (base * count + (outer ^ m)) * part
            out[pl.ds(pl.multiple_of(start, 8), part), :] = source[m][...].astype(F32) * scale


def body(queries, key_rows, value_rows, cotangent, out_weight, lengths, upweight):
    rows = queries.shape[1]
    width = queries.shape[2]
    seq_count = lax.axis_size("seq")
    doc_count = lax.axis_size("doc")
    group = WINDOW // rows
    plane = group * rows
    cols = width // group
    pairs = cols // PAIR
    outer_count = seq_count // group
    units = group * pairs
    span = rows + 2 * WINDOW
    fast = doc_count == 2 and outer_count == 4 and group == 4
    scale = 1.0 / math.sqrt(rows * seq_count * doc_count)

    def inner_swap(value, m):
        return lax.ppermute(value, "seq", [(i, i ^ m) for i in range(seq_count)])

    def outer_swap(value, m):
        return lax.ppermute(value, "seq", [(i, i ^ (m * group)) for i in range(seq_count)])

    def outer_shift(value, step):
        pairs_of = [(i, i + step * group) for i in range(seq_count)]
        return lax.ppermute(value, "seq", [(a, b) for a, b in pairs_of if 0 <= b < seq_count])

    packed = call(
        functools.partial(pack_kernel, group),
        [((2 * rows, cols), BF16)] * group + [((rows, cols), BF16)] * group + [((rows, width), BF16)],
        (lengths, upweight, queries[0], key_rows[0], value_rows[0], cotangent[0]),
        scalars=2, flops=1 << 20, moved=4 << 20,
    )
    own_kv = [packed[0]] + [None] * (group - 1)
    order = list(range(group - 1, 0, -1))
    for m in order:
        own_kv[m] = inner_swap(packed[m], m)
    before = [outer_shift(own_kv[m], 1) for m in range(group)]
    after = [outer_shift(own_kv[m], -1) for m in range(group)]
    q_in = [packed[group]] + [inner_swap(packed[group + m], m) for m in range(1, group)]
    grads = {0: packed[2 * group]}
    step = group // 2
    while step > 0:
        grads.update({m | step: inner_swap(piece, step) for m, piece in grads.items()})
        step //= 2
    grads = [grads[m] for m in range(group)]
    if fast:
        near = out_weight
        far = lax.ppermute(out_weight, "doc", [(0, 1), (1, 0)])
    else:
        whole = lax.all_gather(out_weight, "doc", axis=0, tiled=True)
        near, far = whole[: width // 2], whole[width // 2 :]

    keys, vals, keys_t, query_all, att_t, stats, *att_pieces = call(
        functools.partial(forward_kernel, group),
        [((3 * plane, cols), BF16)] * 2
        + [((cols, 3 * plane), BF16), ((plane, cols), BF16), ((cols, plane), BF16)]
        + [((units, 8, 2 * rows), F32)]
        + [((rows, cols), BF16)] * group,
        (lengths, *q_in, *own_kv, *before, *after),
        scalars=1,
        scratch=[pltpu.VMEM((cols, 3 * plane), BF16), pltpu.VMEM((plane, cols), BF16)],
        flops=4 << 30, moved=4 << 20, vmem=32,
    )
    middle_out = (
        [((cols // outer_count, width), BF16)] * outer_count if fast else [((cols, width), F32)]
    )
    grad_att, *weight_parts = call(
        functools.partial(middle_kernel, group, fast),
        [((plane, cols), BF16)] + middle_out,
        (lengths, att_t, near, far, *grads),
        scalars=1,
        scratch=[
            pltpu.VMEM((plane, width), BF16),
            pltpu.VMEM((cols, width), BF16),
            pltpu.VMEM((cols, width), BF16),
        ],
        flops=1 << 30, moved=4 << 20,
    )

    if fast:
        swapped = [weight_parts[0]] + [outer_swap(weight_parts[m], m) for m in range(1, outer_count)]
        line = sum(part.astype(F32) for part in swapped).astype(BF16)
        half = group // 2
        flat = [(d, i) for d in range(doc_count) for i in range(seq_count)]
        first_pairs, second_pairs = [], []
        for d, i in flat:
            owner = (i % group) // half
            source = d * seq_count + i
            if d == owner:
                first_pairs.append((source, d * seq_count + (i ^ half)))
            else:
                first_pairs.append((source, owner * seq_count + i))
                second_pairs.append((source, owner * seq_count + (i ^ half)))
        got_first = lax.ppermute(line, ("doc", "seq"), first_pairs)
        got_second = lax.ppermute(line, ("doc", "seq"), second_pairs)
        inner = lax.axis_index("seq") % group
        is_owner = inner // half == lax.axis_index("doc")
        final = (
            got_first.astype(F32) + jnp.where(is_owner, line, got_second).astype(F32)
        ).astype(BF16)
        near_parts = [final] + [outer_swap(final, m) for m in range(1, outer_count)]
        far_parts = [inner_swap(part, 1) for part in near_parts]
        (grad_weight,) = call(
            functools.partial(finish_kernel, group, outer_count, scale),
            [((width // doc_count, width), F32)],
            (*near_parts, *far_parts), flops=1 << 20, moved=4 << 20,
        )
    else:
        inner = lax.axis_index("seq") % group
        placed = lax.dynamic_update_slice_in_dim(
            jnp.zeros((width, width), F32), weight_parts[0], inner * cols, 0
        )
        block = lax.psum_scatter(placed, "doc", scatter_dimension=0, tiled=True)
        grad_weight = lax.psum(block, "seq") * scale

    returned = []
    for pair in range(pairs):
        to_before, own, to_after, grad_query = call(
            functools.partial(backward_kernel, group, pair, pairs),
            [((2 * plane, PAIR), BF16), ((2 * plane, PAIR), F32), ((2 * plane, PAIR), BF16)]
            + [((plane, PAIR), BF16)],
            (lengths, keys, vals, keys_t, query_all, grad_att, stats),
            scalars=1,
            scratch=[pltpu.VMEM((3 * plane, PAIR), F32)] * 2,
            flops=4 << 30, moved=4 << 20, vmem=32,
        )
        from_after = outer_shift(to_before, -1)
        from_before = outer_shift(to_after, 1)
        pieces = call(
            functools.partial(settle_kernel, group),
            [((3 * rows, PAIR), BF16)] * group,
            (own, from_after, from_before, grad_query), flops=1 << 20, moved=2 << 20,
        )
        returned += [pieces[0]] + [inner_swap(pieces[m], m) for m in range(1, group)]
    grads_out = call(
        functools.partial(unpack_kernel, group),
        [((rows, width), BF16)] * 3,
        tuple(returned), flops=1 << 20, moved=2 << 20,
    )
    att_in = [att_pieces[0]] + [inner_swap(att_pieces[m], m) for m in range(1, group)]
    (layer_out,) = call(
        functools.partial(project_kernel, group, fast),
        [((rows, width), BF16)],
        (near, far, *att_in),
        scratch=[pltpu.VMEM((rows, width), BF16)],
        flops=1 << 30, moved=4 << 20,
    )
    grad_query, grad_key, grad_value = grads_out
    return (layer_out[None], grad_query[None], grad_key[None], grad_value[None], grad_weight)


def solution(mesh):
    spec = P("doc", "seq", None)
    return jax.shard_map(
        body,
        mesh=mesh,
        in_specs=(spec, spec, spec, spec, P("doc", None), P("doc", None), P("doc", None)),
        out_specs=(spec, spec, spec, spec, P("doc", None)),
        check_vma=False,
    )
```

```python
import functools
import math

import jax
import jax.numpy as jnp
from jax import lax
from jax.experimental import pallas as pl
from jax.experimental.pallas import tpu as pltpu
from jax.sharding import PartitionSpec as P

HEADS = 16
HEAD_DIM = 64
WINDOW = 512
BLOCK = 64
DOCS = 4
PAIR = 2 * HEAD_DIM
MASKED = -1e30
BF16 = jnp.bfloat16
F32 = jnp.float32

VMEM = pl.BlockSpec(memory_space=pltpu.VMEM)
HBM = pl.BlockSpec(memory_space=pltpu.HBM)
ANY = pl.BlockSpec(memory_space=pl.ANY)
SMEM = pl.BlockSpec(memory_space=pltpu.SMEM)


def call(kernel, out_shape, operands, hbm=0, after=(), scratch=(), flops=0, moved=0, vmem=24):
    outs = [jax.ShapeDtypeStruct(shape, kind) for shape, kind in out_shape]
    operands = [
        pltpu.with_memory_space_constraint(value, pltpu.HBM) if i < hbm else value
        for i, value in enumerate(operands)
    ]
    count = len(operands)

    def run(*refs):
        kernel(*refs[:count], *refs[count + len(after) :])

    return pl.pallas_call(
        run,
        out_shape=outs,
        in_specs=[HBM] * hbm + [VMEM] * (count - hbm) + [ANY] * len(after),
        out_specs=[VMEM] * len(outs),
        scratch_shapes=list(scratch),
        compiler_params=pltpu.CompilerParams(vmem_limit_bytes=vmem << 20),
        cost_estimate=pl.CostEstimate(flops=flops, bytes_accessed=moved, transcendentals=0),
    )(*operands, *after)


def dot_nn(a, b):
    return lax.dot_general(a, b, (((1,), (0,)), ((), ())), preferred_element_type=F32)


def dot_nt(a, b):
    return lax.dot_general(a, b, (((1,), (1,)), ((), ())), preferred_element_type=F32)


def doc_bounds(len_ref):
    ends = []
    total = 0
    for d in range(DOCS):
        total = total + len_ref[0, d] * BLOCK
        ends.append(total)
    return ends


def query_limits(len_ref, first, count):
    ends = doc_bounds(len_ref)
    query = first + lax.broadcasted_iota(jnp.int32, (1, count), 1)
    low = jnp.zeros((1, count), jnp.int32)
    high = jnp.full((1, count), ends[DOCS - 1], jnp.int32)
    for d in range(DOCS - 1):
        low = jnp.where(query >= ends[d], ends[d], low)
        high = jnp.where(query < ends[DOCS - 2 - d], ends[DOCS - 2 - d], high)
    return jnp.maximum(low, query - WINDOW), jnp.minimum(high, query + WINDOW + 1)


def pack_kernel(group, fast, len_hbm, up_hbm, k_hbm, v_hbm, q_hbm, cot_hbm, weight_hbm, *refs):
    own_kv, far_kv, own_rest, near_all, far_rest = (
        refs[0], refs[1 : group - 1], refs[group - 1], refs[group], refs[group + 1 : 2 * group - 1]
    )
    limits = refs[2 * group - 1]
    k_ref, v_ref, q_ref, cot_ref, len_ref, up_ref, sems = refs[-7:]
    copies = [(len_hbm, len_ref), (up_hbm, up_ref), (k_hbm, k_ref), (v_hbm, v_ref)]
    copies += [(q_hbm, q_ref), (cot_hbm, cot_ref)]
    rows = q_ref.shape[0]
    cols = q_ref.shape[1] // group
    place = lax.axis_index("seq")
    inner = lax.rem(place, group)
    if fast:
        start = pl.multiple_of(lax.rem(inner, 2) * cols, 128)
        copies += [(weight_hbm.at[pl.ds(start, cols)], refs[2 * group])]
    loads = [
        pltpu.make_async_copy(source, target, sems.at[i])
        for i, (source, target) in enumerate(copies)
    ]
    for load in loads:
        load.start()
    starts = [pl.multiple_of((inner ^ m) * cols, 128) for m in range(group)]
    loads[2].wait()
    loads[3].wait()
    for m, target in ((0, own_kv), (1, near_all), *((m, far_kv[m - 2]) for m in range(2, group))):
        target[0:rows, :] = k_ref[:, pl.ds(starts[m], cols)]
        target[rows : 2 * rows, :] = v_ref[:, pl.ds(starts[m], cols)]
    loads[0].wait()
    loads[1].wait()
    ends = doc_bounds(len_ref)
    low, high = query_limits(len_ref, (place - inner) * rows, group * rows)
    limits[0:1, :] = low
    limits[1:2, :] = high
    pos = place * rows + lax.broadcasted_iota(jnp.int32, (rows, 1), 0)
    factor = jnp.full((rows, 1), up_ref[0, 0], jnp.int32)
    for d in range(1, DOCS):
        factor = jnp.where(pos >= ends[d - 1], up_ref[0, d], factor)
    loads[4].wait()
    own_rest[0:rows, :] = q_ref[:, pl.ds(starts[0], cols)]
    near_all[2 * rows : 3 * rows, :] = q_ref[:, pl.ds(starts[1], cols)]
    for m in range(2, group):
        far_rest[m - 2][0:rows, :] = q_ref[:, pl.ds(starts[m], cols)]
    loads[5].wait()
    weighted = (factor.astype(F32) * cot_ref[...].astype(F32)).astype(BF16)
    for j in range(group):
        part = weighted[:, j * cols : (j + 1) * cols]
        own_rest[(j + 1) * rows : (j + 2) * rows, :] = part
        near_all[(j + 3) * rows : (j + 4) * rows, :] = part
        far_rest[0][(j + 1) * rows : (j + 2) * rows, :] = part
    if fast:
        loads[6].wait()


def join_kernel(parts, *refs):
    passed = (len(refs) - parts - 1) // 2
    out = refs[parts + passed]
    size = out.shape[0] // parts
    for m, source in enumerate(refs[:parts]):
        out[m * size : (m + 1) * size, :] = source[0:size, :]
    for source, target in zip(refs[parts : parts + passed], refs[parts + passed + 1 :]):
        target[...] = source[...]


def key_bias(limits, plane_start, block, rows, span):
    at = slice(block * rows, (block + 1) * rows)
    first = plane_start + (block * rows - WINDOW)
    key = first + lax.broadcasted_iota(jnp.int32, (span, rows), 0)
    seen = (key >= limits[0:1, at]) & (key < limits[1:2, at])
    bias = jnp.where(seen, 0.0, MASKED).astype(F32)
    return jnp.concatenate([bias, bias], axis=1)


def stack_pair(block):
    lane = lax.broadcasted_iota(jnp.int32, block.shape, 1)
    zero = jnp.zeros_like(block)
    return jnp.concatenate(
        [jnp.where(lane < HEAD_DIM, block, zero), jnp.where(lane < HEAD_DIM, zero, block)], axis=0
    )


def unstack_pair(both, rows):
    return jnp.concatenate([both[:HEAD_DIM, :rows], both[HEAD_DIM:, rows:]], axis=0)


LOG2_SCALE = math.log2(math.e) * HEAD_DIM ** (-0.5)


def forward_kernel(group, limits, *refs):
    own_kv, near_all = refs[0], refs[1]
    far_kv = refs[2:group]
    own_rest = refs[group]
    far_rest = refs[group + 1 : 2 * group - 1]
    sides = refs[2 * group - 1 : 2 * group + 1]
    keys, vals, keys_t, queries, att_t, att, stats, vals_t = refs[2 * group + 1 :]
    rows, cols = far_rest[-1].shape
    plane = group * rows
    span = rows + 2 * WINDOW
    place = lax.axis_index("seq")
    inner = lax.rem(place, group)
    plane_start = (place - inner) * rows
    even = 1 - lax.rem(place // group, 2)
    for m in range(group):
        spot = (inner ^ m) * rows
        asked = (own_rest, 0) if m == 0 else (near_all, 2 * rows) if m == 1 else (far_rest[m - 2], 0)
        at = pl.ds(pl.multiple_of(spot, 128), rows)
        queries[at, :] = asked[0][asked[1] : asked[1] + rows, :]
        held = own_kv if m == 0 else near_all if m == 1 else far_kv[m - 2]
        base = m * 2 * rows
        sources = [(held, 0, 1), (sides[0], base, 2 * even), (sides[1], base, 2 - 2 * even)]
        for source, base, side in sources:
            at = pl.ds(pl.multiple_of(side * plane + spot, 128), rows)
            keys[at, :] = source[base : base + rows, :]
            vals[at, :] = source[base + rows : base + 2 * rows, :]
    keys_t[...] = keys[...].T
    vals_t[...] = vals[...].T
    for block in range(group):
        bias = key_bias(limits, plane_start, block, rows, span)
        at = slice(block * rows, (block + 1) * rows)
        seen = slice(block * rows, block * rows + span)
        for pair in range(cols // PAIR):
            lanes = slice(pair * PAIR, (pair + 1) * PAIR)
            score = dot_nt(keys[seen, lanes], stack_pair(queries[at, lanes])) + bias
            peak = jnp.max(score, axis=0, keepdims=True)
            power = jnp.exp2((score - peak) * LOG2_SCALE)
            share = 1.0 / jnp.sum(power, axis=0, keepdims=True)
            unit = block * (cols // PAIR) + pair
            stats[unit, 0:1, :] = peak
            stats[unit, 1:2, :] = share
            prob = (power * share).astype(BF16)
            mixed = unstack_pair(dot_nn(vals_t[lanes, seen], prob), rows).astype(BF16)
            att_t[lanes, at] = mixed
            att[at, lanes] = mixed.T


def middle_kernel(group, fast, att_t, near, far, *refs):
    grads = refs[:group]
    grad_att = refs[group]
    out = refs[group + 1 : -3]
    grad_all, weight, total = refs[-3:]
    rows = grad_all.shape[0] // group
    cols = att_t.shape[0]
    place = lax.axis_index("seq")
    inner = lax.rem(place, group)
    if fast:
        is_near = inner // 2 == lax.axis_index("doc")

        @pl.when(is_near)
        def _():
            weight[...] = near[...]

        @pl.when(jnp.logical_not(is_near))
        def _():
            weight[...] = far[...]

    else:
        weight[...] = near[...]
    for m in range(group):
        skipped = grads[m].shape[0] - group * rows
        for j in range(group):
            grad_all[
                pl.ds(pl.multiple_of((inner ^ m) * rows, 128), rows), j * cols : (j + 1) * cols
            ] = grads[m][skipped + j * rows : skipped + (j + 1) * rows, :]
    product = dot_nn(att_t[...], grad_all[...])
    if fast:
        total[...] = product.astype(BF16)
        count = len(out)
        part = cols // count
        outer = place // group
        for m in range(count):
            out[m][...] = total[pl.ds(pl.multiple_of((outer ^ m) * part, 16), part), :]
    else:
        out[0][...] = product
    grad_att[...] = dot_nt(grad_all[...], weight[...]).astype(BF16)


def backward_kernel(
    group, limits, keys, vals, keys_t, queries, grad_att, stats,
    to_first, own, to_second, grad_query, key_sum, value_sum,
):
    plane, cols = queries.shape
    rows = plane // group
    span = rows + 2 * WINDOW
    pairs = cols // PAIR
    place = lax.axis_index("seq")
    plane_start = (place - lax.rem(place, group)) * rows
    key_sum[...] = jnp.zeros_like(key_sum)
    value_sum[...] = jnp.zeros_like(value_sum)
    for block in range(group):
        bias = key_bias(limits, plane_start, block, rows, span)
        at = slice(block * rows, (block + 1) * rows)
        seen = slice(block * rows, block * rows + span)
        for pair in range(pairs):
            lanes = slice(pair * PAIR, (pair + 1) * PAIR)
            unit = block * pairs + pair
            query = stack_pair(queries[at, lanes])
            grad = stack_pair(grad_att[at, lanes])
            score = dot_nt(keys[seen, lanes], query) + bias
            prob = jnp.exp2((score - stats[unit, 0:1, :]) * LOG2_SCALE) * stats[unit, 1:2, :]
            grad_prob = dot_nt(vals[seen, lanes], grad)
            centre = jnp.sum(prob * grad_prob, axis=0, keepdims=True)
            grad_score = (prob * (grad_prob - centre) * HEAD_DIM ** (-0.5)).astype(BF16)
            value_sum[seen, lanes] += dot_nn(prob.astype(BF16), grad)
            key_sum[seen, lanes] += dot_nn(grad_score, query)
            turned = unstack_pair(dot_nn(keys_t[lanes, seen], grad_score), rows)
            grad_query[at, lanes] = turned.astype(BF16).T
    even = 1 - lax.rem(place // group, 2)
    for target, side in ((to_first, 2 * even), (own, 1), (to_second, 2 - 2 * even)):
        kept = pl.ds(pl.multiple_of(side * plane, 128), plane)
        target[0:plane, :] = key_sum[kept, :].astype(target.dtype)
        target[plane : 2 * plane, :] = value_sum[kept, :].astype(target.dtype)


def settle_kernel(group, own, from_first, from_second, grad_query, att, *pieces):
    plane = grad_query.shape[0]
    rows = plane // group
    inner = lax.rem(lax.axis_index("seq"), group)
    for m in range(group):
        spot = (inner ^ m) * rows
        mine = pl.ds(pl.multiple_of(spot, 128), rows)
        pieces[m][0:rows, :] = grad_query[mine, :]
        for part in range(2):
            at = pl.ds(pl.multiple_of(part * plane + spot, 128), rows)
            summed = own[at, :] + from_first[at, :].astype(F32) + from_second[at, :].astype(F32)
            pieces[m][(part + 1) * rows : (part + 2) * rows, :] = summed.astype(BF16)
        pieces[m][3 * rows : 4 * rows, :] = att[mine, :]


def unpack_kernel(group, fast, near, far, farther, *refs):
    pieces, outs, out, att = refs[:group], refs[group : group + 3], refs[group + 3], refs[group + 4]
    rows, width = out.shape
    cols = width // group
    half = width // 2
    inner = lax.rem(lax.axis_index("seq"), group)
    first = lax.axis_index("doc") if fast else 0
    for m in range(group):
        at = pl.ds(pl.multiple_of((inner ^ m) * cols, 128), cols)
        for part in range(3):
            outs[part][:, at] = pieces[m][part * rows : (part + 1) * rows, :]
        att[:, at] = pieces[m][3 * rows : 4 * rows, :]
    total = dot_nn(att[:, pl.ds(pl.multiple_of(first * half, 128), half)], near[...])
    for side, weight in ((0, far), (1, farther)):
        start = (1 - first) * half + (lax.rem(inner, 2) ^ side) * cols
        total += dot_nn(att[:, pl.ds(pl.multiple_of(start, 128), cols)], weight[...])
    out[...] = total.astype(BF16)


def finish_kernel(group, count, scale, *refs):
    out = refs[-1]
    near, far = refs[:count], refs[count : 2 * count]
    place = lax.axis_index("seq")
    side = lax.rem(place, 2)
    outer = place // group
    part = near[0].shape[0]
    for source, base in ((near, side), (far, 1 - side)):
        for m in range(count):
            start = (base * count + (outer ^ m)) * part
            out[pl.ds(pl.multiple_of(start, 8), part), :] = source[m][...].astype(F32) * scale


def body(queries, key_rows, value_rows, cotangent, out_weight, lengths, upweight):
    rows = queries.shape[1]
    width = queries.shape[2]
    seq_count = lax.axis_size("seq")
    doc_count = lax.axis_size("doc")
    group = WINDOW // rows
    plane = group * rows
    cols = width // group
    pairs = cols // PAIR
    outer_count = seq_count // group
    units = group * pairs
    span = rows + 2 * WINDOW
    fast = doc_count == 2 and outer_count == 4
    scale = 1.0 / math.sqrt(rows * seq_count * doc_count)

    def inner_swap(value, m):
        return lax.ppermute(value, "seq", [(i, i ^ m) for i in range(seq_count)])

    def outer_swap(value, m):
        return lax.ppermute(value, "seq", [(i, i ^ (m * group)) for i in range(seq_count)])

    def outer_first(value):
        return outer_swap(value, 1)

    def outer_second(value):
        pairs_of = [(i, (((i // group + 1) ^ 1) - 1) * group + i % group) for i in range(seq_count)]
        return lax.ppermute(value, "seq", [(a, b) for a, b in pairs_of if 0 <= b < seq_count])

    tokens = (rows, width)
    rest = [(((1 + group) * rows, cols), BF16), ((rows, cols), BF16)]
    chunk = [((cols, width), BF16)] if fast else []
    own_kv, *packed = call(
        functools.partial(pack_kernel, group, fast),
        [((2 * rows, cols), BF16)] * (group - 1)
        + [rest[0], (((3 + group) * rows, cols), BF16), *rest]
        + [((8, plane), jnp.int32), *chunk],
        (lengths, upweight, key_rows[0], value_rows[0], queries[0], cotangent[0], out_weight),
        hbm=7,
        scratch=[pltpu.VMEM(tokens, BF16)] * 4
        + [pltpu.SMEM((1, DOCS), jnp.int32)] * 2
        + [pltpu.SemaphoreType.DMA((7,))],
        flops=1 << 20, moved=4 << 20,
    )
    far_kv = [inner_swap(packed[m - 2], m) for m in range(2, group)]
    own_rest, near_all, rest_first, rest_last, limits, *weight = packed[group - 2 :]
    near_all = inner_swap(near_all, 1)
    joined, rest_first, rest_last, *weight = call(
        functools.partial(join_kernel, group),
        [((2 * group * rows, cols), BF16), *rest, *chunk],
        (own_kv, near_all, *far_kv, rest_first, rest_last, *weight),
        flops=1 << 20, moved=1 << 20,
    )
    sides = [outer_first(joined), outer_second(joined)]
    far_rest = [inner_swap(rest_first, 2), inner_swap(rest_last, 3)]
    grads = [own_rest, near_all, far_rest[0], inner_swap(far_rest[0], 1)]
    inner = lax.axis_index("seq") % group
    if fast:
        near, half_near = weight[0], out_weight
        far = lax.ppermute(near, "doc", [(0, 1), (1, 0)])
        half_far = [far, inner_swap(far, 1)]
    else:
        whole = lax.all_gather(out_weight, "doc", axis=0, tiled=True)
        chunks = [lax.dynamic_slice_in_dim(whole, at * cols, cols, 0) for at in (
            inner, 2 + inner % 2, 2 + (inner + 1) % 2
        )]
        near = far = chunks[0]
        half_near, half_far = whole[: width // 2], chunks[1:]

    keys, vals, keys_t, query_all, att_t, att, stats = call(
        functools.partial(forward_kernel, group),
        [((3 * plane, cols), BF16)] * 2
        + [((cols, 3 * plane), BF16), ((plane, cols), BF16), ((cols, plane), BF16)]
        + [((plane, cols), BF16), ((units, 8, 2 * rows), F32)],
        (limits, own_kv, near_all, *far_kv, own_rest, *far_rest, *sides),
        scratch=[pltpu.VMEM((cols, 3 * plane), BF16)],
        flops=4 << 30, moved=4 << 20, vmem=32,
    )
    middle_out = (
        [((cols // outer_count, width), BF16)] * outer_count if fast else [((cols, width), F32)]
    )
    grad_att, *weight_parts = call(
        functools.partial(middle_kernel, group, fast),
        [((plane, cols), BF16)] + middle_out,
        (att_t, near, far, *grads),
        scratch=[
            pltpu.VMEM((plane, width), BF16),
            pltpu.VMEM((cols, width), BF16),
            pltpu.VMEM((cols, width), BF16),
        ],
        flops=1 << 30, moved=4 << 20,
    )

    if fast:
        swapped = [weight_parts[0]] + [outer_swap(weight_parts[m], m) for m in range(1, outer_count)]
        line = sum(part.astype(F32) for part in swapped).astype(BF16)
        flat = [(d, i) for d in range(doc_count) for i in range(seq_count)]
        first_pairs, second_pairs = [], []
        for d, i in flat:
            owner = (i % group) // 2
            source = d * seq_count + i
            if d == owner:
                first_pairs.append((source, d * seq_count + (i ^ 2)))
            else:
                first_pairs.append((source, owner * seq_count + i))
                second_pairs.append((source, owner * seq_count + (i ^ 2)))
        got_first = lax.ppermute(line, ("doc", "seq"), first_pairs)
        got_second = lax.ppermute(line, ("doc", "seq"), second_pairs)
        is_owner = inner // 2 == lax.axis_index("doc")
        final = (
            got_first.astype(F32) + jnp.where(is_owner, line, got_second).astype(F32)
        ).astype(BF16)
        before_settle = (final,)
        near_parts = [final] + [outer_swap(final, m) for m in range(1, outer_count)]
        far_parts = [inner_swap(part, 1) for part in near_parts]
        (grad_weight,) = call(
            functools.partial(finish_kernel, group, outer_count, scale),
            [((width // doc_count, width), F32)],
            (*near_parts, *far_parts), flops=1 << 20, moved=4 << 20,
        )
    else:
        placed = lax.dynamic_update_slice_in_dim(
            jnp.zeros((width, width), F32), weight_parts[0], inner * cols, 0
        )
        block = lax.psum_scatter(placed, "doc", scatter_dimension=0, tiled=True)
        grad_weight = lax.psum(block, "seq") * scale
        before_settle = ()

    to_first, own, to_second, grad_query = call(
        functools.partial(backward_kernel, group),
        [((2 * plane, cols), BF16), ((2 * plane, cols), F32), ((2 * plane, cols), BF16)]
        + [((plane, cols), BF16)],
        (limits, keys, vals, keys_t, query_all, grad_att, stats),
        after=half_far[1:],
        scratch=[pltpu.VMEM((3 * plane, cols), F32)] * 2,
        flops=8 << 30, moved=4 << 20, vmem=32,
    )
    pieces = call(
        functools.partial(settle_kernel, group),
        [((4 * rows, cols), BF16)] * group,
        (own, outer_first(to_first), outer_second(to_second), grad_query, att),
        after=before_settle, flops=1 << 20, moved=2 << 20,
    )
    pieces = [pieces[0]] + [inner_swap(pieces[m], m) for m in range(1, group)]
    grad_query, grad_key, grad_value, layer_out = call(
        functools.partial(unpack_kernel, group, fast),
        [((rows, width), BF16)] * 4,
        (half_near, *half_far, *pieces),
        scratch=[pltpu.VMEM((rows, width), BF16)],
        flops=1 << 30, moved=4 << 20,
    )
    return (layer_out[None], grad_query[None], grad_key[None], grad_value[None], grad_weight)


def solution(mesh):
    spec = P("doc", "seq", None)
    return jax.shard_map(
        body,
        mesh=mesh,
        in_specs=(spec, spec, spec, spec, P("doc", None), P("doc", None), P("doc", None)),
        out_specs=(spec, spec, spec, spec, P("doc", None)),
        check_vma=False,
    )
```

```python
import functools
import math

import jax
import jax.numpy as jnp
from jax import lax
from jax.experimental import pallas as pl
from jax.experimental.pallas import tpu as pltpu
from jax.sharding import PartitionSpec as P

HEADS = 16
HEAD_DIM = 64
WINDOW = 512
BLOCK = 64
DOCS = 4
PAIR = 2 * HEAD_DIM
MASKED = -1e30
BF16 = jnp.bfloat16
F32 = jnp.float32

VMEM = pl.BlockSpec(memory_space=pltpu.VMEM)
HBM = pl.BlockSpec(memory_space=pltpu.HBM)
ANY = pl.BlockSpec(memory_space=pl.ANY)
SMEM = pl.BlockSpec(memory_space=pltpu.SMEM)


def call(kernel, out_shape, operands, hbm=0, after=(), scratch=(), flops=0, moved=0, vmem=24):
    outs = [jax.ShapeDtypeStruct(shape, kind) for shape, kind in out_shape]
    operands = [
        pltpu.with_memory_space_constraint(value, pltpu.HBM) if i < hbm else value
        for i, value in enumerate(operands)
    ]
    count = len(operands)

    def run(*refs):
        kernel(*refs[:count], *refs[count + len(after) :])

    return pl.pallas_call(
        run,
        out_shape=outs,
        in_specs=[HBM] * hbm + [VMEM] * (count - hbm) + [ANY] * len(after),
        out_specs=[VMEM] * len(outs),
        scratch_shapes=list(scratch),
        compiler_params=pltpu.CompilerParams(vmem_limit_bytes=vmem << 20),
        cost_estimate=pl.CostEstimate(flops=flops, bytes_accessed=moved, transcendentals=0),
    )(*operands, *after)


def dot_nn(a, b):
    return lax.dot_general(a, b, (((1,), (0,)), ((), ())), preferred_element_type=F32)


def dot_nt(a, b):
    return lax.dot_general(a, b, (((1,), (1,)), ((), ())), preferred_element_type=F32)


def doc_bounds(len_ref):
    ends = []
    total = 0
    for d in range(DOCS):
        total = total + len_ref[0, d] * BLOCK
        ends.append(total)
    return ends


def query_limits(len_ref, first, count):
    ends = doc_bounds(len_ref)
    query = first + lax.broadcasted_iota(jnp.int32, (1, count), 1)
    low = jnp.zeros((1, count), jnp.int32)
    high = jnp.full((1, count), ends[DOCS - 1], jnp.int32)
    for d in range(DOCS - 1):
        low = jnp.where(query >= ends[d], ends[d], low)
        high = jnp.where(query < ends[DOCS - 2 - d], ends[DOCS - 2 - d], high)
    return jnp.maximum(low, query - WINDOW), jnp.minimum(high, query + WINDOW + 1)


def pack_kernel(group, fast, len_hbm, up_hbm, k_hbm, v_hbm, q_hbm, cot_hbm, weight_hbm, *refs):
    own_kv, far_kv, own_rest, near_all, far_rest = (
        refs[0], refs[1 : group - 1], refs[group - 1], refs[group], refs[group + 1 : 2 * group - 1]
    )
    limits = refs[2 * group - 1]
    k_ref, v_ref, q_ref, cot_ref, len_ref, up_ref, sems = refs[-7:]
    copies = [(len_hbm, len_ref), (up_hbm, up_ref), (k_hbm, k_ref), (v_hbm, v_ref)]
    copies += [(q_hbm, q_ref), (cot_hbm, cot_ref)]
    rows = q_ref.shape[0]
    cols = q_ref.shape[1] // group
    place = lax.axis_index("seq")
    inner = lax.rem(place, group)
    if fast:
        start = pl.multiple_of(lax.rem(inner, 2) * cols, 128)
        copies += [(weight_hbm.at[pl.ds(start, cols)], refs[2 * group])]
    loads = [
        pltpu.make_async_copy(source, target, sems.at[i])
        for i, (source, target) in enumerate(copies)
    ]
    for load in loads:
        load.start()
    starts = [pl.multiple_of((inner ^ m) * cols, 128) for m in range(group)]
    loads[2].wait()
    loads[3].wait()
    for m, target in ((0, own_kv), (1, near_all), *((m, far_kv[m - 2]) for m in range(2, group))):
        target[0:rows, :] = k_ref[:, pl.ds(starts[m], cols)]
        target[rows : 2 * rows, :] = v_ref[:, pl.ds(starts[m], cols)]
    loads[0].wait()
    loads[1].wait()
    ends = doc_bounds(len_ref)
    low, high = query_limits(len_ref, (place - inner) * rows, group * rows)
    limits[0:1, :] = low
    limits[1:2, :] = high
    pos = place * rows + lax.broadcasted_iota(jnp.int32, (rows, 1), 0)
    factor = jnp.full((rows, 1), up_ref[0, 0], jnp.int32)
    for d in range(1, DOCS):
        factor = jnp.where(pos >= ends[d - 1], up_ref[0, d], factor)
    loads[4].wait()
    own_rest[0:rows, :] = q_ref[:, pl.ds(starts[0], cols)]
    near_all[2 * rows : 3 * rows, :] = q_ref[:, pl.ds(starts[1], cols)]
    for m in range(2, group):
        far_rest[m - 2][0:rows, :] = q_ref[:, pl.ds(starts[m], cols)]
    loads[5].wait()
    weighted = (factor.astype(F32) * cot_ref[...].astype(F32)).astype(BF16)
    for j in range(group):
        part = weighted[:, j * cols : (j + 1) * cols]
        own_rest[(j + 1) * rows : (j + 2) * rows, :] = part
        near_all[(j + 3) * rows : (j + 4) * rows, :] = part
        far_rest[0][(j + 1) * rows : (j + 2) * rows, :] = part
    if fast:
        loads[6].wait()


def join_kernel(parts, *refs):
    passed = (len(refs) - parts - 1) // 2
    out = refs[parts + passed]
    size = out.shape[0] // parts
    for m, source in enumerate(refs[:parts]):
        out[m * size : (m + 1) * size, :] = source[0:size, :]
    for source, target in zip(refs[parts : parts + passed], refs[parts + passed + 1 :]):
        target[...] = source[...]


def key_bias(limits, plane_start, block, rows, span):
    at = slice(block * rows, (block + 1) * rows)
    first = plane_start + (block * rows - WINDOW)
    key = first + lax.broadcasted_iota(jnp.int32, (span, rows), 0)
    seen = (key >= limits[0:1, at]) & (key < limits[1:2, at])
    bias = jnp.where(seen, 0.0, MASKED).astype(F32)
    return jnp.concatenate([bias, bias], axis=1)


def stack_pair(block):
    lane = lax.broadcasted_iota(jnp.int32, block.shape, 1)
    zero = jnp.zeros_like(block)
    return jnp.concatenate(
        [jnp.where(lane < HEAD_DIM, block, zero), jnp.where(lane < HEAD_DIM, zero, block)], axis=0
    )


def unstack_pair(both, rows):
    return jnp.concatenate([both[:HEAD_DIM, :rows], both[HEAD_DIM:, rows:]], axis=0)


def unit_slices(unit, pairs, rows, span):
    block, pair = unit // pairs, unit % pairs
    return (
        slice(block * rows, (block + 1) * rows),
        slice(block * rows, block * rows + span),
        slice(pair * PAIR, (pair + 1) * PAIR),
    )


LOG2_SCALE = math.log2(math.e) * HEAD_DIM ** (-0.5)


def forward_kernel(group, limits, *refs):
    own_kv, near_all = refs[0], refs[1]
    far_kv = refs[2:group]
    own_rest = refs[group]
    far_rest = refs[group + 1 : 2 * group - 1]
    sides = refs[2 * group - 1 : 2 * group + 1]
    keys, vals, keys_t, queries, att_t, att, stats, vals_t = refs[2 * group + 1 :]
    rows, cols = far_rest[-1].shape
    plane = group * rows
    span = rows + 2 * WINDOW
    place = lax.axis_index("seq")
    inner = lax.rem(place, group)
    plane_start = (place - inner) * rows
    even = 1 - lax.rem(place // group, 2)
    for m in range(group):
        spot = (inner ^ m) * rows
        asked = (own_rest, 0) if m == 0 else (near_all, 2 * rows) if m == 1 else (far_rest[m - 2], 0)
        at = pl.ds(pl.multiple_of(spot, 128), rows)
        queries[at, :] = asked[0][asked[1] : asked[1] + rows, :]
        held = own_kv if m == 0 else near_all if m == 1 else far_kv[m - 2]
        base = m * 2 * rows
        sources = [(held, 0, 1), (sides[0], base, 2 * even), (sides[1], base, 2 - 2 * even)]
        for source, base, side in sources:
            at = pl.ds(pl.multiple_of(side * plane + spot, 128), rows)
            keys[at, :] = source[base : base + rows, :]
            vals[at, :] = source[base + rows : base + 2 * rows, :]
    keys_t[...] = keys[...].T
    vals_t[...] = vals[...].T
    pairs = cols // PAIR
    count = group * pairs

    def scored(unit, bias):
        at, seen, lanes = unit_slices(unit, pairs, rows, span)
        return dot_nt(keys[seen, lanes], stack_pair(queries[at, lanes])) + bias

    def mix(unit, prob):
        at, seen, lanes = unit_slices(unit, pairs, rows, span)
        mixed = unstack_pair(dot_nn(vals_t[lanes, seen], prob), rows).astype(BF16)
        att_t[lanes, at] = mixed
        att[at, lanes] = mixed.T

    bias = key_bias(limits, plane_start, 0, rows, span)
    ahead = scored(0, bias)
    prob = None
    for unit in range(count):
        score = ahead
        if unit + 1 < count:
            if (unit + 1) % pairs == 0:
                bias = key_bias(limits, plane_start, (unit + 1) // pairs, rows, span)
            ahead = scored(unit + 1, bias)
        if unit > 0:
            mix(unit - 1, prob)
        peak = jnp.max(score, axis=0, keepdims=True)
        power = jnp.exp2((score - peak) * LOG2_SCALE)
        share = 1.0 / jnp.sum(power, axis=0, keepdims=True)
        stats[unit, 0:1, :] = peak
        stats[unit, 1:2, :] = share
        prob = (power * share).astype(BF16)
    mix(count - 1, prob)


def middle_kernel(group, fast, att_t, near, far, *refs):
    grads = refs[:group]
    grad_att = refs[group]
    out = refs[group + 1 : -3]
    grad_all, weight, total = refs[-3:]
    rows = grad_all.shape[0] // group
    cols = att_t.shape[0]
    place = lax.axis_index("seq")
    inner = lax.rem(place, group)
    if fast:
        is_near = inner // 2 == lax.axis_index("doc")

        @pl.when(is_near)
        def _():
            weight[...] = near[...]

        @pl.when(jnp.logical_not(is_near))
        def _():
            weight[...] = far[...]

    else:
        weight[...] = near[...]
    for m in range(group):
        skipped = grads[m].shape[0] - group * rows
        for j in range(group):
            grad_all[
                pl.ds(pl.multiple_of((inner ^ m) * rows, 128), rows), j * cols : (j + 1) * cols
            ] = grads[m][skipped + j * rows : skipped + (j + 1) * rows, :]
    product = dot_nn(att_t[...], grad_all[...])
    if fast:
        total[...] = product.astype(BF16)
        count = len(out)
        part = cols // count
        outer = place // group
        for m in range(count):
            out[m][...] = total[pl.ds(pl.multiple_of((outer ^ m) * part, 16), part), :]
    else:
        out[0][...] = product
    grad_att[...] = dot_nt(grad_all[...], weight[...]).astype(BF16)


def backward_kernel(
    group, limits, keys, vals, keys_t, queries, grad_att, stats, att,
    to_first, own, to_second, *refs,
):
    mine, near, far, key_sum, value_sum, grad_query = refs
    plane, cols = queries.shape
    rows = plane // group
    span = rows + 2 * WINDOW
    pairs = cols // PAIR
    count = group * pairs
    place = lax.axis_index("seq")
    inner = lax.rem(place, group)
    plane_start = (place - inner) * rows
    key_sum[...] = jnp.zeros_like(key_sum)
    value_sum[...] = jnp.zeros_like(value_sum)

    def begin(unit, bias):
        at, seen, lanes = unit_slices(unit, pairs, rows, span)
        query = stack_pair(queries[at, lanes])
        grad = stack_pair(grad_att[at, lanes])
        score = dot_nt(keys[seen, lanes], query) + bias
        return query, grad, score, dot_nt(vals[seen, lanes], grad)

    def end(unit, query, grad, prob, grad_score):
        at, seen, lanes = unit_slices(unit, pairs, rows, span)
        value_sum[seen, lanes] += dot_nn(prob, grad)
        key_sum[seen, lanes] += dot_nn(grad_score, query)
        turned = unstack_pair(dot_nn(keys_t[lanes, seen], grad_score), rows)
        grad_query[at, lanes] = turned.astype(BF16).T

    bias = key_bias(limits, plane_start, 0, rows, span)
    ahead = begin(0, bias)
    behind = None
    for unit in range(count):
        query, grad, score, grad_prob = ahead
        if unit + 1 < count:
            if (unit + 1) % pairs == 0:
                bias = key_bias(limits, plane_start, (unit + 1) // pairs, rows, span)
            ahead = begin(unit + 1, bias)
        if unit > 0:
            end(unit - 1, *behind)
        prob = jnp.exp2((score - stats[unit, 0:1, :]) * LOG2_SCALE) * stats[unit, 1:2, :]
        centre = jnp.sum(prob * grad_prob, axis=0, keepdims=True)
        grad_score = (prob * (grad_prob - centre) * HEAD_DIM ** (-0.5)).astype(BF16)
        behind = (query, grad, prob.astype(BF16), grad_score)
    end(count - 1, *behind)
    for m, (target, base) in enumerate(((mine, 0), (near, 0), (far, 0), (far, 2 * rows))):
        taken = pl.ds(pl.multiple_of((inner ^ m) * rows, 128), rows)
        target[base : base + rows, :] = grad_query[taken, :]
        target[base + rows : base + 2 * rows, :] = att[taken, :]
    even = 1 - lax.rem(place // group, 2)
    for target, side in ((to_first, 2 * even), (own, 1), (to_second, 2 - 2 * even)):
        kept = pl.ds(pl.multiple_of(side * plane, 128), plane)
        target[0:plane, :] = key_sum[kept, :].astype(target.dtype)
        target[plane : 2 * plane, :] = value_sum[kept, :].astype(target.dtype)


def settle_kernel(group, own, from_first, from_second, near, far, *pieces):
    rows = pieces[0].shape[0] // 2
    plane = group * rows
    inner = lax.rem(lax.axis_index("seq"), group)
    for m in range(group):
        spot = (inner ^ m) * rows
        for part in range(2):
            at = pl.ds(pl.multiple_of(part * plane + spot, 128), rows)
            summed = own[at, :] + from_first[at, :].astype(F32) + from_second[at, :].astype(F32)
            pieces[m][part * rows : (part + 1) * rows, :] = summed.astype(BF16)
    pieces[1][2 * rows : 4 * rows, :] = near[...]
    pieces[1][4 * rows : 6 * rows, :] = far[2 * rows : 4 * rows, :]


def unpack_kernel(group, fast, near, far, farther, *refs):
    sums, mine, early = refs[:group], refs[group], refs[group + 1]
    outs, out, att = refs[group + 2 : group + 5], refs[group + 5], refs[group + 6]
    rows, width = out.shape
    cols = width // group
    half = width // 2
    inner = lax.rem(lax.axis_index("seq"), group)
    first = lax.axis_index("doc") if fast else 0
    held = ((mine, 0), (sums[1], 2 * rows), (early, 0), (sums[1], 4 * rows))
    for m in range(group):
        at = pl.ds(pl.multiple_of((inner ^ m) * cols, 128), cols)
        outs[1][:, at] = sums[m][0:rows, :]
        outs[2][:, at] = sums[m][rows : 2 * rows, :]
        source, base = held[m]
        outs[0][:, at] = source[base : base + rows, :]
        att[:, at] = source[base + rows : base + 2 * rows, :]
    total = dot_nn(att[:, pl.ds(pl.multiple_of(first * half, 128), half)], near[...])
    for side, weight in ((0, far), (1, farther)):
        start = (1 - first) * half + (lax.rem(inner, 2) ^ side) * cols
        total += dot_nn(att[:, pl.ds(pl.multiple_of(start, 128), cols)], weight[...])
    out[...] = total.astype(BF16)


def add_kernel(*refs):
    total = refs[0][...].astype(F32)
    for ref in refs[1:-1]:
        total += ref[...].astype(F32)
    refs[-1][...] = total.astype(BF16)


def pass_kernel(source, target):
    target[...] = source[...]


def cross_kernel(group, own, first, second, out):
    inner = lax.rem(lax.axis_index("seq"), group)
    owner = inner // 2 == lax.axis_index("doc")

    @pl.when(owner)
    def _():
        out[...] = (first[...].astype(F32) + own[...].astype(F32)).astype(BF16)

    @pl.when(jnp.logical_not(owner))
    def _():
        out[...] = (first[...].astype(F32) + second[...].astype(F32)).astype(BF16)


def gather_kernel(group, *refs):
    out = refs[-1]
    outer = lax.axis_index("seq") // group
    part = refs[0].shape[0]
    for m, source in enumerate(refs[:-1]):
        out[pl.ds(pl.multiple_of((outer ^ m) * part, 16), part), :] = source[...]


def finish_kernel(scale, near, far, out):
    side = lax.rem(lax.axis_index("seq"), 2)
    size = near.shape[0]
    for source, base in ((near, side), (far, 1 - side)):
        at = pl.ds(pl.multiple_of(base * size, 128), size)
        out[at, :] = source[...].astype(F32) * scale


def body(queries, key_rows, value_rows, cotangent, out_weight, lengths, upweight):
    rows = queries.shape[1]
    width = queries.shape[2]
    seq_count = lax.axis_size("seq")
    doc_count = lax.axis_size("doc")
    group = WINDOW // rows
    plane = group * rows
    cols = width // group
    pairs = cols // PAIR
    outer_count = seq_count // group
    units = group * pairs
    span = rows + 2 * WINDOW
    fast = doc_count == 2 and outer_count == 4
    scale = 1.0 / math.sqrt(rows * seq_count * doc_count)

    def inner_swap(value, m):
        return lax.ppermute(value, "seq", [(i, i ^ m) for i in range(seq_count)])

    def outer_swap(value, m):
        return lax.ppermute(value, "seq", [(i, i ^ (m * group)) for i in range(seq_count)])

    def outer_first(value):
        return outer_swap(value, 1)

    def outer_second(value):
        pairs_of = [(i, (((i // group + 1) ^ 1) - 1) * group + i % group) for i in range(seq_count)]
        return lax.ppermute(value, "seq", [(a, b) for a, b in pairs_of if 0 <= b < seq_count])

    tokens = (rows, width)
    rest = [(((1 + group) * rows, cols), BF16), ((rows, cols), BF16)]
    chunk = [((cols, width), BF16)] if fast else []
    own_kv, *packed = call(
        functools.partial(pack_kernel, group, fast),
        [((2 * rows, cols), BF16)] * (group - 1)
        + [rest[0], (((3 + group) * rows, cols), BF16), *rest]
        + [((8, plane), jnp.int32), *chunk],
        (lengths, upweight, key_rows[0], value_rows[0], queries[0], cotangent[0], out_weight),
        hbm=7,
        scratch=[pltpu.VMEM(tokens, BF16)] * 4
        + [pltpu.SMEM((1, DOCS), jnp.int32)] * 2
        + [pltpu.SemaphoreType.DMA((7,))],
        flops=1 << 20, moved=4 << 20,
    )
    far_kv = [inner_swap(packed[m - 2], m) for m in range(2, group)]
    own_rest, near_all, rest_first, rest_last, limits, *weight = packed[group - 2 :]
    near_all = inner_swap(near_all, 1)
    joined, rest_first, rest_last = call(
        functools.partial(join_kernel, group),
        [((2 * group * rows, cols), BF16), *rest],
        (own_kv, near_all, *far_kv, rest_first, rest_last),
        flops=1 << 20, moved=1 << 20,
    )
    sides = [outer_first(joined), outer_second(joined)]
    far_rest = [inner_swap(rest_first, 2), inner_swap(rest_last, 3)]
    grads = [own_rest, near_all, far_rest[0], inner_swap(far_rest[0], 1)]
    inner = lax.axis_index("seq") % group
    if fast:
        near, half_near = weight[0], out_weight
        far = lax.ppermute(near, "doc", [(0, 1), (1, 0)])
        half_far = [far, inner_swap(far, 1)]
    else:
        whole = lax.all_gather(out_weight, "doc", axis=0, tiled=True)
        chunks = [lax.dynamic_slice_in_dim(whole, at * cols, cols, 0) for at in (
            inner, 2 + inner % 2, 2 + (inner + 1) % 2
        )]
        near = far = chunks[0]
        half_near, half_far = whole[: width // 2], chunks[1:]

    keys, vals, keys_t, query_all, att_t, att, stats = call(
        functools.partial(forward_kernel, group),
        [((3 * plane, cols), BF16)] * 2
        + [((cols, 3 * plane), BF16), ((plane, cols), BF16), ((cols, plane), BF16)]
        + [((plane, cols), BF16), ((units, 8, 2 * rows), F32)],
        (limits, own_kv, near_all, *far_kv, own_rest, *far_rest, *sides),
        scratch=[pltpu.VMEM((cols, 3 * plane), BF16)],
        flops=4 << 30, moved=4 << 20, vmem=32,
    )
    middle_out = (
        [((cols // outer_count, width), BF16)] * outer_count if fast else [((cols, width), F32)]
    )
    grad_att, *weight_parts = call(
        functools.partial(middle_kernel, group, fast),
        [((plane, cols), BF16)] + middle_out,
        (att_t, near, far, *grads),
        scratch=[
            pltpu.VMEM((plane, width), BF16),
            pltpu.VMEM((cols, width), BF16),
            pltpu.VMEM((cols, width), BF16),
        ],
        flops=1 << 30, moved=4 << 20,
    )

    to_first, own, to_second, early_own, early_near, early_far = call(
        functools.partial(backward_kernel, group),
        [((2 * plane, cols), BF16), ((2 * plane, cols), F32), ((2 * plane, cols), BF16)]
        + [((2 * rows, cols), BF16)] * 2
        + [((4 * rows, cols), BF16)],
        (limits, keys, vals, keys_t, query_all, grad_att, stats, att),
        after=half_far[1:],
        scratch=[pltpu.VMEM((3 * plane, cols), F32)] * 2 + [pltpu.VMEM((plane, cols), BF16)],
        flops=8 << 30, moved=4 << 20, vmem=32,
    )
    if fast:
        swapped = [weight_parts[0]] + [outer_swap(weight_parts[m], m) for m in range(1, outer_count)]
        part_shape = [(swapped[0].shape, BF16)]
        (line,) = call(
            add_kernel, part_shape, swapped, after=(early_near,), flops=1 << 18, moved=1 << 19
        )
        (early_far,) = call(
            pass_kernel, [(early_far.shape, BF16)], (early_far,), after=(line,),
            flops=1 << 18, moved=1 << 19,
        )
        flat = [(d, i) for d in range(doc_count) for i in range(seq_count)]
        first_pairs, second_pairs = [], []
        for d, i in flat:
            owner = (i % group) // 2
            source = d * seq_count + i
            if d == owner:
                first_pairs.append((source, d * seq_count + (i ^ 2)))
            else:
                first_pairs.append((source, owner * seq_count + i))
                second_pairs.append((source, owner * seq_count + (i ^ 2)))
        got_first = lax.ppermute(line, ("doc", "seq"), first_pairs)
        got_second = lax.ppermute(line, ("doc", "seq"), second_pairs)
        early = inner_swap(early_far, 2)
        (final,) = call(
            functools.partial(cross_kernel, group), part_shape, (line, got_first, got_second), after=(early,),
            flops=2 << 30, moved=1 << 19,
        )
        gathered = [final] + [outer_swap(final, m) for m in range(1, outer_count)]
        before_settle = gathered[:1]
    else:
        placed = lax.dynamic_update_slice_in_dim(
            jnp.zeros((width, width), F32), weight_parts[0], inner * cols, 0
        )
        block = lax.psum_scatter(placed, "doc", scatter_dimension=0, tiled=True)
        grad_weight = lax.psum(block, "seq") * scale
        before_settle = ()
        early = inner_swap(early_far, 2)

    sums = call(
        functools.partial(settle_kernel, group),
        [(((6 if m == 1 else 2) * rows, cols), BF16) for m in range(group)],
        (own, outer_first(to_first), outer_second(to_second), early_near, early),
        after=before_settle, flops=10 << 30, moved=2 << 20,
    )
    sums = [sums[0]] + [inner_swap(sums[m], m) for m in range(1, group)]
    if fast:
        (gathered,) = call(
            functools.partial(gather_kernel, group), [((cols, width), BF16)], gathered,
            after=sums[2:], flops=1 << 18, moved=1 << 20,
        )
        (grad_weight,) = call(
            functools.partial(finish_kernel, scale), [((width // doc_count, width), F32)],
            (gathered, inner_swap(gathered, 1)), flops=1 << 20, moved=4 << 20,
        )
    grad_query, grad_key, grad_value, layer_out = call(
        functools.partial(unpack_kernel, group, fast),
        [((rows, width), BF16)] * 4,
        (half_near, *half_far, *sums, early_own, early),
        scratch=[pltpu.VMEM((rows, width), BF16)],
        flops=1 << 30, moved=4 << 20,
    )
    return (layer_out[None], grad_query[None], grad_key[None], grad_value[None], grad_weight)


def solution(mesh):
    spec = P("doc", "seq", None)
    return jax.shard_map(
        body,
        mesh=mesh,
        in_specs=(spec, spec, spec, spec, P("doc", None), P("doc", None), P("doc", None)),
        out_specs=(spec, spec, spec, spec, P("doc", None)),
        check_vma=False,
    )
```

```python
import functools
import math

import jax
import jax.numpy as jnp
from jax import lax
from jax.experimental import pallas as pl
from jax.experimental.pallas import tpu as pltpu
from jax.sharding import PartitionSpec as P

HEADS = 16
HEAD_DIM = 64
WINDOW = 512
BLOCK = 64
DOCS = 4
PAIR = 2 * HEAD_DIM
MASKED = -1e30
BF16 = jnp.bfloat16
F32 = jnp.float32

VMEM = pl.BlockSpec(memory_space=pltpu.VMEM)
HBM = pl.BlockSpec(memory_space=pltpu.HBM)
ANY = pl.BlockSpec(memory_space=pl.ANY)
SMEM = pl.BlockSpec(memory_space=pltpu.SMEM)


def call(kernel, out_shape, operands, hbm=0, after=(), scratch=(), flops=0, moved=0, vmem=24):
    outs = [jax.ShapeDtypeStruct(shape, kind) for shape, kind in out_shape]
    operands = [
        pltpu.with_memory_space_constraint(value, pltpu.HBM) if i < hbm else value
        for i, value in enumerate(operands)
    ]
    count = len(operands)

    def run(*refs):
        kernel(*refs[:count], *refs[count + len(after) :])

    return pl.pallas_call(
        run,
        out_shape=outs,
        in_specs=[HBM] * hbm + [VMEM] * (count - hbm) + [ANY] * len(after),
        out_specs=[VMEM] * len(outs),
        scratch_shapes=list(scratch),
        compiler_params=pltpu.CompilerParams(vmem_limit_bytes=vmem << 20),
        cost_estimate=pl.CostEstimate(flops=flops, bytes_accessed=moved, transcendentals=0),
    )(*operands, *after)


def dot_nn(a, b):
    return lax.dot_general(a, b, (((1,), (0,)), ((), ())), preferred_element_type=F32)


def dot_nt(a, b):
    return lax.dot_general(a, b, (((1,), (1,)), ((), ())), preferred_element_type=F32)


def doc_bounds(len_ref):
    ends = []
    total = 0
    for d in range(DOCS):
        total = total + len_ref[0, d] * BLOCK
        ends.append(total)
    return ends


def query_limits(len_ref, first, count):
    ends = doc_bounds(len_ref)
    query = first + lax.broadcasted_iota(jnp.int32, (1, count), 1)
    low = jnp.zeros((1, count), jnp.int32)
    high = jnp.full((1, count), ends[DOCS - 1], jnp.int32)
    for d in range(DOCS - 1):
        low = jnp.where(query >= ends[d], ends[d], low)
        high = jnp.where(query < ends[DOCS - 2 - d], ends[DOCS - 2 - d], high)
    return jnp.maximum(low, query - WINDOW), jnp.minimum(high, query + WINDOW + 1)


def pack_kernel(group, fast, len_hbm, up_hbm, k_hbm, v_hbm, q_hbm, cot_hbm, weight_hbm, *refs):
    own_kv, far_kv, own_rest, near_all, far_rest = (
        refs[0], refs[1 : group - 1], refs[group - 1], refs[group], refs[group + 1 : 2 * group - 1]
    )
    limits = refs[2 * group - 1]
    k_ref, v_ref, q_ref, cot_ref, len_ref, up_ref, sems = refs[-7:]
    copies = [(len_hbm, len_ref), (up_hbm, up_ref), (k_hbm, k_ref), (v_hbm, v_ref)]
    copies += [(q_hbm, q_ref), (cot_hbm, cot_ref)]
    rows = q_ref.shape[0]
    cols = q_ref.shape[1] // group
    place = lax.axis_index("seq")
    inner = lax.rem(place, group)
    if fast:
        start = pl.multiple_of(lax.rem(inner, 2) * cols, 128)
        copies += [(weight_hbm.at[pl.ds(start, cols)], refs[2 * group])]
    loads = [
        pltpu.make_async_copy(source, target, sems.at[i])
        for i, (source, target) in enumerate(copies)
    ]
    for load in loads:
        load.start()
    starts = [pl.multiple_of((inner ^ m) * cols, 128) for m in range(group)]
    loads[2].wait()
    loads[3].wait()
    for m, target in ((0, own_kv), (1, near_all), *((m, far_kv[m - 2]) for m in range(2, group))):
        target[0:rows, :] = k_ref[:, pl.ds(starts[m], cols)]
        target[rows : 2 * rows, :] = v_ref[:, pl.ds(starts[m], cols)]
    loads[0].wait()
    loads[1].wait()
    ends = doc_bounds(len_ref)
    low, high = query_limits(len_ref, (place - inner) * rows, group * rows)
    limits[0:1, :] = low
    limits[1:2, :] = high
    pos = place * rows + lax.broadcasted_iota(jnp.int32, (rows, 1), 0)
    factor = jnp.full((rows, 1), up_ref[0, 0], jnp.int32)
    for d in range(1, DOCS):
        factor = jnp.where(pos >= ends[d - 1], up_ref[0, d], factor)
    loads[4].wait()
    own_rest[0:rows, :] = q_ref[:, pl.ds(starts[0], cols)]
    near_all[2 * rows : 3 * rows, :] = q_ref[:, pl.ds(starts[1], cols)]
    for m in range(2, group):
        far_rest[m - 2][0:rows, :] = q_ref[:, pl.ds(starts[m], cols)]
    loads[5].wait()
    weighted = (factor.astype(F32) * cot_ref[...].astype(F32)).astype(BF16)
    for j in range(group):
        part = weighted[:, j * cols : (j + 1) * cols]
        own_rest[(j + 1) * rows : (j + 2) * rows, :] = part
        near_all[(j + 3) * rows : (j + 4) * rows, :] = part
        far_rest[0][(j + 1) * rows : (j + 2) * rows, :] = part
    if fast:
        loads[6].wait()


def join_kernel(*refs):
    out = refs[-1]
    size = out.shape[0] // (len(refs) - 1)
    for m, source in enumerate(refs[:-1]):
        out[m * size : (m + 1) * size, :] = source[0:size, :]


def pass_kernel(*refs):
    half = len(refs) // 2
    for source, target in zip(refs[:half], refs[half:]):
        target[...] = source[...]


def key_bias(limits, plane_start, block, rows, span):
    at = slice(block * rows, (block + 1) * rows)
    first = plane_start + (block * rows - WINDOW)
    key = first + lax.broadcasted_iota(jnp.int32, (span, rows), 0)
    seen = (key >= limits[0:1, at]) & (key < limits[1:2, at])
    bias = jnp.where(seen, 0.0, MASKED).astype(F32)
    return jnp.concatenate([bias, bias], axis=1)


def stack_pair(block):
    lane = lax.broadcasted_iota(jnp.int32, block.shape, 1)
    zero = jnp.zeros_like(block)
    return jnp.concatenate(
        [jnp.where(lane < HEAD_DIM, block, zero), jnp.where(lane < HEAD_DIM, zero, block)], axis=0
    )


def unstack_pair(both, rows):
    return jnp.concatenate([both[:HEAD_DIM, :rows], both[HEAD_DIM:, rows:]], axis=0)


def unit_slices(unit, pairs, rows, span):
    block, pair = unit // pairs, unit % pairs
    return (
        slice(block * rows, (block + 1) * rows),
        slice(block * rows, block * rows + span),
        slice(pair * PAIR, (pair + 1) * PAIR),
    )


LOG2_SCALE = math.log2(math.e) * HEAD_DIM ** (-0.5)


def forward_kernel(group, limits, *refs):
    own_kv, near_all = refs[0], refs[1]
    far_kv = refs[2:group]
    own_rest = refs[group]
    far_rest = refs[group + 1 : 2 * group - 1]
    sides = refs[2 * group - 1 : 2 * group + 3]
    keys, vals, keys_t, queries, att_t, att, stats, vals_t = refs[2 * group + 3 :]
    rows, cols = far_rest[-1].shape
    plane = group * rows
    span = rows + 2 * WINDOW
    place = lax.axis_index("seq")
    inner = lax.rem(place, group)
    plane_start = (place - inner) * rows
    even = 1 - lax.rem(place // group, 2)
    for m in range(group):
        spot = (inner ^ m) * rows
        asked = (own_rest, 0) if m == 0 else (near_all, 2 * rows) if m == 1 else (far_rest[m - 2], 0)
        at = pl.ds(pl.multiple_of(spot, 128), rows)
        queries[at, :] = asked[0][asked[1] : asked[1] + rows, :]
        held = own_kv if m == 0 else near_all if m == 1 else far_kv[m - 2]
        first, second = sides[0:2] if m == 0 else sides[2:4]
        base = max(m - 1, 0) * 2 * rows
        sources = [(held, 0, 1), (first, base, 2 * even), (second, base, 2 - 2 * even)]
        for source, base, side in sources:
            at = pl.ds(pl.multiple_of(side * plane + spot, 128), rows)
            keys[at, :] = source[base : base + rows, :]
            vals[at, :] = source[base + rows : base + 2 * rows, :]
    keys_t[...] = keys[...].T
    vals_t[...] = vals[...].T
    pairs = cols // PAIR
    count = group * pairs

    def scored(unit, bias):
        at, seen, lanes = unit_slices(unit, pairs, rows, span)
        return dot_nt(keys[seen, lanes], stack_pair(queries[at, lanes])) + bias

    def mix(unit, prob):
        at, seen, lanes = unit_slices(unit, pairs, rows, span)
        mixed = unstack_pair(dot_nn(vals_t[lanes, seen], prob), rows).astype(BF16)
        att_t[lanes, at] = mixed
        att[at, lanes] = mixed.T

    bias = key_bias(limits, plane_start, 0, rows, span)
    ahead = scored(0, bias)
    prob = None
    for unit in range(count):
        score = ahead
        if unit + 1 < count:
            if (unit + 1) % pairs == 0:
                bias = key_bias(limits, plane_start, (unit + 1) // pairs, rows, span)
            ahead = scored(unit + 1, bias)
        if unit > 0:
            mix(unit - 1, prob)
        peak = jnp.max(score, axis=0, keepdims=True)
        power = jnp.exp2((score - peak) * LOG2_SCALE)
        share = 1.0 / jnp.sum(power, axis=0, keepdims=True)
        stats[unit, 0:1, :] = peak
        stats[unit, 1:2, :] = share
        prob = (power * share).astype(BF16)
    mix(count - 1, prob)


def middle_kernel(group, fast, att_t, near, far, *refs):
    grads = refs[:group]
    grad_att = refs[group]
    out = refs[group + 1 : -3]
    grad_all, weight, total = refs[-3:]
    rows = grad_all.shape[0] // group
    cols = att_t.shape[0]
    place = lax.axis_index("seq")
    inner = lax.rem(place, group)
    if fast:
        is_near = inner // 2 == lax.axis_index("doc")

        @pl.when(is_near)
        def _():
            weight[...] = near[...]

        @pl.when(jnp.logical_not(is_near))
        def _():
            weight[...] = far[...]

    else:
        weight[...] = near[...]
    for m in range(group):
        skipped = grads[m].shape[0] - group * rows
        for j in range(group):
            grad_all[
                pl.ds(pl.multiple_of((inner ^ m) * rows, 128), rows), j * cols : (j + 1) * cols
            ] = grads[m][skipped + j * rows : skipped + (j + 1) * rows, :]
    product = dot_nn(att_t[...], grad_all[...])
    if fast:
        total[...] = product.astype(BF16)
        count = len(out)
        part = cols // count
        outer = place // group
        for m in range(count):
            out[m][...] = total[pl.ds(pl.multiple_of((outer ^ m) * part, 16), part), :]
    else:
        out[0][...] = product
    grad_att[...] = dot_nt(grad_all[...], weight[...]).astype(BF16)


def backward_kernel(
    group, limits, keys, vals, keys_t, queries, grad_att, stats, att,
    to_first, own, to_second, *refs,
):
    mine, near, far, key_sum, value_sum, grad_query = refs
    plane, cols = queries.shape
    rows = plane // group
    span = rows + 2 * WINDOW
    pairs = cols // PAIR
    count = group * pairs
    place = lax.axis_index("seq")
    inner = lax.rem(place, group)
    plane_start = (place - inner) * rows
    key_sum[...] = jnp.zeros_like(key_sum)
    value_sum[...] = jnp.zeros_like(value_sum)

    def begin(unit, bias):
        at, seen, lanes = unit_slices(unit, pairs, rows, span)
        query = stack_pair(queries[at, lanes])
        grad = stack_pair(grad_att[at, lanes])
        score = dot_nt(keys[seen, lanes], query) + bias
        return query, grad, score, dot_nt(vals[seen, lanes], grad)

    def end(unit, query, grad, prob, grad_score):
        at, seen, lanes = unit_slices(unit, pairs, rows, span)
        value_sum[seen, lanes] += dot_nn(prob, grad)
        key_sum[seen, lanes] += dot_nn(grad_score, query)
        turned = unstack_pair(dot_nn(keys_t[lanes, seen], grad_score), rows)
        grad_query[at, lanes] = turned.astype(BF16).T

    bias = key_bias(limits, plane_start, 0, rows, span)
    ahead = begin(0, bias)
    behind = None
    for unit in range(count):
        query, grad, score, grad_prob = ahead
        if unit + 1 < count:
            if (unit + 1) % pairs == 0:
                bias = key_bias(limits, plane_start, (unit + 1) // pairs, rows, span)
            ahead = begin(unit + 1, bias)
        if unit > 0:
            end(unit - 1, *behind)
        prob = jnp.exp2((score - stats[unit, 0:1, :]) * LOG2_SCALE) * stats[unit, 1:2, :]
        centre = jnp.sum(prob * grad_prob, axis=0, keepdims=True)
        grad_score = (prob * (grad_prob - centre) * HEAD_DIM ** (-0.5)).astype(BF16)
        behind = (query, grad, prob.astype(BF16), grad_score)
    end(count - 1, *behind)
    for m, (target, base) in enumerate(((mine, 0), (near, 0), (far, 0), (far, 2 * rows))):
        taken = pl.ds(pl.multiple_of((inner ^ m) * rows, 128), rows)
        target[base : base + rows, :] = grad_query[taken, :]
        target[base + rows : base + 2 * rows, :] = att[taken, :]
    even = 1 - lax.rem(place // group, 2)
    for target, side in ((to_first, 2 * even), (own, 1), (to_second, 2 - 2 * even)):
        kept = pl.ds(pl.multiple_of(side * plane, 128), plane)
        target[0:plane, :] = key_sum[kept, :].astype(target.dtype)
        target[plane : 2 * plane, :] = value_sum[kept, :].astype(target.dtype)


def settle_kernel(group, own, from_first, from_second, *pieces):
    rows = pieces[0].shape[0] // 2
    plane = group * rows
    inner = lax.rem(lax.axis_index("seq"), group)
    for m in range(group):
        spot = (inner ^ m) * rows
        for part in range(2):
            at = pl.ds(pl.multiple_of(part * plane + spot, 128), rows)
            summed = own[at, :] + from_first[at, :].astype(F32) + from_second[at, :].astype(F32)
            pieces[m][part * rows : (part + 1) * rows, :] = summed.astype(BF16)


def relay_kernel(near, far, out):
    size = near.shape[0]
    out[0:size, :] = near[...]
    out[size : 2 * size, :] = far[size : 2 * size, :]


def unpack_kernel(group, *refs):
    pieces, outs = refs[:group], refs[group:]
    rows, width = outs[0].shape
    cols = width // group
    inner = lax.rem(lax.axis_index("seq"), group)
    for m in range(group):
        at = pl.ds(pl.multiple_of((inner ^ m) * cols, 128), cols)
        for part in range(2):
            outs[part][:, at] = pieces[m][part * rows : (part + 1) * rows, :]


def project_kernel(group, fast, near, far, farther, mine, early, relayed, grad_query, out, done, att):
    rows, width = out.shape
    cols = width // group
    half = width // 2
    inner = lax.rem(lax.axis_index("seq"), group)
    first = lax.axis_index("doc") if fast else 0
    held = ((mine, 0), (relayed, 0), (early, 0), (relayed, 2 * rows))
    for m in range(group):
        at = pl.ds(pl.multiple_of((inner ^ m) * cols, 128), cols)
        source, base = held[m]
        grad_query[:, at] = source[base : base + rows, :]
        att[:, at] = source[base + rows : base + 2 * rows, :]
    total = dot_nn(att[:, pl.ds(pl.multiple_of(first * half, 128), half)], near[...])
    for side, weight in ((0, far), (1, farther)):
        start = (1 - first) * half + (lax.rem(inner, 2) ^ side) * cols
        total += dot_nn(att[:, pl.ds(pl.multiple_of(start, 128), cols)], weight[...])
    out[...] = total.astype(BF16)
    done[...] = jnp.zeros_like(done)


def add_kernel(*refs):
    total = refs[0][...].astype(F32)
    for ref in refs[1:-1]:
        total += ref[...].astype(F32)
    refs[-1][...] = total.astype(BF16)


def cross_kernel(group, own, first, second, out):
    inner = lax.rem(lax.axis_index("seq"), group)
    owner = inner // 2 == lax.axis_index("doc")

    @pl.when(owner)
    def _():
        out[...] = (first[...].astype(F32) + own[...].astype(F32)).astype(BF16)

    @pl.when(jnp.logical_not(owner))
    def _():
        out[...] = (first[...].astype(F32) + second[...].astype(F32)).astype(BF16)


def gather_kernel(group, *refs):
    out = refs[-1]
    outer = lax.axis_index("seq") // group
    part = refs[0].shape[0]
    for m, source in enumerate(refs[:-1]):
        out[pl.ds(pl.multiple_of((outer ^ m) * part, 16), part), :] = source[...]


def finish_kernel(scale, near, far, out):
    side = lax.rem(lax.axis_index("seq"), 2)
    size = near.shape[0]
    for source, base in ((near, side), (far, 1 - side)):
        at = pl.ds(pl.multiple_of(base * size, 128), size)
        out[at, :] = source[...].astype(F32) * scale


def body(queries, key_rows, value_rows, cotangent, out_weight, lengths, upweight):
    rows = queries.shape[1]
    width = queries.shape[2]
    seq_count = lax.axis_size("seq")
    doc_count = lax.axis_size("doc")
    group = WINDOW // rows
    plane = group * rows
    cols = width // group
    pairs = cols // PAIR
    outer_count = seq_count // group
    units = group * pairs
    span = rows + 2 * WINDOW
    fast = doc_count == 2 and outer_count == 4
    scale = 1.0 / math.sqrt(rows * seq_count * doc_count)

    def inner_swap(value, m):
        return lax.ppermute(value, "seq", [(i, i ^ m) for i in range(seq_count)])

    def outer_swap(value, m):
        return lax.ppermute(value, "seq", [(i, i ^ (m * group)) for i in range(seq_count)])

    def outer_first(value):
        return outer_swap(value, 1)

    def outer_second(value):
        pairs_of = [(i, (((i // group + 1) ^ 1) - 1) * group + i % group) for i in range(seq_count)]
        return lax.ppermute(value, "seq", [(a, b) for a, b in pairs_of if 0 <= b < seq_count])

    tokens = (rows, width)
    rest = [(((1 + group) * rows, cols), BF16), ((rows, cols), BF16)]
    chunk = [((cols, width), BF16)] if fast else []
    own_kv, *packed = call(
        functools.partial(pack_kernel, group, fast),
        [((2 * rows, cols), BF16)] * (group - 1)
        + [rest[0], (((3 + group) * rows, cols), BF16), *rest]
        + [((8, plane), jnp.int32), *chunk],
        (lengths, upweight, key_rows[0], value_rows[0], queries[0], cotangent[0], out_weight),
        hbm=7,
        scratch=[pltpu.VMEM(tokens, BF16)] * 4
        + [pltpu.SMEM((1, DOCS), jnp.int32)] * 2
        + [pltpu.SemaphoreType.DMA((7,))],
        flops=1 << 20, moved=4 << 20,
    )
    far_kv = [inner_swap(packed[m - 2], m) for m in range(2, group)]
    own_rest, near_all, rest_first, rest_last, limits, *weight = packed[group - 2 :]
    near_all = inner_swap(near_all, 1)
    (sent_kv,) = call(
        pass_kernel, [((2 * rows, cols), BF16)], (own_kv,), flops=3 << 30, moved=1 << 18
    )
    sides = [outer_first(sent_kv), outer_second(sent_kv)]
    rest_first, rest_last = call(
        pass_kernel, rest, (rest_first, rest_last),
        after=(near_all, *far_kv), flops=1 << 18, moved=1 << 20,
    )
    far_rest = [inner_swap(rest_first, 2), inner_swap(rest_last, 3)]
    (joined,) = call(
        join_kernel, [((2 * (group - 1) * rows, cols), BF16)], (near_all, *far_kv),
        after=(rest_last, *sides), flops=3 << 30, moved=1 << 20,
    )
    sides += [outer_first(joined), outer_second(joined)]
    grads = [own_rest, near_all, far_rest[0], inner_swap(far_rest[0], 1)]
    inner = lax.axis_index("seq") % group
    if fast:
        near, half_near = weight[0], out_weight
        far = lax.ppermute(near, "doc", [(0, 1), (1, 0)])
        half_far = [far, inner_swap(far, 1)]
    else:
        whole = lax.all_gather(out_weight, "doc", axis=0, tiled=True)
        chunks = [lax.dynamic_slice_in_dim(whole, at * cols, cols, 0) for at in (
            inner, 2 + inner % 2, 2 + (inner + 1) % 2
        )]
        near = far = chunks[0]
        half_near, half_far = whole[: width // 2], chunks[1:]

    keys, vals, keys_t, query_all, att_t, att, stats = call(
        functools.partial(forward_kernel, group),
        [((3 * plane, cols), BF16)] * 2
        + [((cols, 3 * plane), BF16), ((plane, cols), BF16), ((cols, plane), BF16)]
        + [((plane, cols), BF16), ((units, 8, 2 * rows), F32)],
        (limits, own_kv, near_all, *far_kv, own_rest, *far_rest, *sides),
        scratch=[pltpu.VMEM((cols, 3 * plane), BF16)],
        flops=4 << 30, moved=4 << 20, vmem=32,
    )
    middle_out = (
        [((cols // outer_count, width), BF16)] * outer_count if fast else [((cols, width), F32)]
    )
    grad_att, *weight_parts = call(
        functools.partial(middle_kernel, group, fast),
        [((plane, cols), BF16)] + middle_out,
        (att_t, near, far, *grads),
        scratch=[
            pltpu.VMEM((plane, width), BF16),
            pltpu.VMEM((cols, width), BF16),
            pltpu.VMEM((cols, width), BF16),
        ],
        flops=1 << 30, moved=4 << 20,
    )

    to_first, own, to_second, early_own, early_near, early_far = call(
        functools.partial(backward_kernel, group),
        [((2 * plane, cols), BF16), ((2 * plane, cols), F32), ((2 * plane, cols), BF16)]
        + [((2 * rows, cols), BF16)] * 2
        + [((4 * rows, cols), BF16)],
        (limits, keys, vals, keys_t, query_all, grad_att, stats, att),
        after=half_far[1:],
        scratch=[pltpu.VMEM((3 * plane, cols), F32)] * 2 + [pltpu.VMEM((plane, cols), BF16)],
        flops=8 << 30, moved=4 << 20, vmem=32,
    )
    if fast:
        swapped = [weight_parts[0]] + [outer_swap(weight_parts[m], m) for m in range(1, outer_count)]
        part_shape = [(swapped[0].shape, BF16)]
        (line,) = call(
            add_kernel, part_shape, swapped, after=(early_near,), flops=1 << 18, moved=1 << 19
        )
        (early_far,) = call(
            pass_kernel, [(early_far.shape, BF16)], (early_far,), after=(swapped[1],),
            flops=2 << 30, moved=1 << 19,
        )
        flat = [(d, i) for d in range(doc_count) for i in range(seq_count)]
        first_pairs, second_pairs = [], []
        for d, i in flat:
            owner = (i % group) // 2
            source = d * seq_count + i
            if d == owner:
                first_pairs.append((source, d * seq_count + (i ^ 2)))
            else:
                first_pairs.append((source, owner * seq_count + i))
                second_pairs.append((source, owner * seq_count + (i ^ 2)))
        got_first = lax.ppermute(line, ("doc", "seq"), first_pairs)
        got_second = lax.ppermute(line, ("doc", "seq"), second_pairs)
        early = inner_swap(early_far, 2)
        (final,) = call(
            functools.partial(cross_kernel, group), part_shape, (line, got_first, got_second), after=(early,),
            flops=2 << 30, moved=1 << 19,
        )
        gathered = [final] + [outer_swap(final, m) for m in range(1, outer_count)]
        before_settle = gathered[:1]
    else:
        placed = lax.dynamic_update_slice_in_dim(
            jnp.zeros((width, width), F32), weight_parts[0], inner * cols, 0
        )
        block = lax.psum_scatter(placed, "doc", scatter_dimension=0, tiled=True)
        grad_weight = lax.psum(block, "seq") * scale
        before_settle = ()
        early = inner_swap(early_far, 2)

    (relayed,) = call(
        relay_kernel, [((4 * rows, cols), BF16)], (early_near, early),
        after=(), flops=1 << 18, moved=1 << 20,
    )
    relayed = inner_swap(relayed, 1)
    grad_query, layer_out, projected = call(
        functools.partial(project_kernel, group, fast),
        [((rows, width), BF16)] * 2 + [((8, 128), F32)],
        (half_near, *half_far, early_own, early, relayed),
        scratch=[pltpu.VMEM((rows, width), BF16)],
        flops=1 << 30, moved=4 << 20,
    )
    sums = call(
        functools.partial(settle_kernel, group),
        [((2 * rows, cols), BF16)] * group,
        (own, outer_first(to_first), outer_second(to_second)),
        after=before_settle, flops=10 << 30, moved=2 << 20,
    )
    sums = [sums[0]] + [inner_swap(sums[m], m) for m in range(1, group)]
    if fast:
        (gathered,) = call(
            functools.partial(gather_kernel, group), [((cols, width), BF16)], gathered,
            after=(*sums[1:], projected), flops=1 << 18, moved=1 << 20,
        )
        (grad_weight,) = call(
            functools.partial(finish_kernel, scale), [((width // doc_count, width), F32)],
            (gathered, inner_swap(gathered, 1)), flops=1 << 20, moved=4 << 20,
        )
    grad_key, grad_value = call(
        functools.partial(unpack_kernel, group), [((rows, width), BF16)] * 2, sums,
        flops=1 << 20, moved=1 << 20,
    )
    return (layer_out[None], grad_query[None], grad_key[None], grad_value[None], grad_weight)


def solution(mesh):
    spec = P("doc", "seq", None)
    return jax.shard_map(
        body,
        mesh=mesh,
        in_specs=(spec, spec, spec, spec, P("doc", None), P("doc", None), P("doc", None)),
        out_specs=(spec, spec, spec, spec, P("doc", None)),
        check_vma=False,
    )
```

```python
import functools
import math

import jax
import jax.numpy as jnp
from jax import lax
from jax.experimental import pallas as pl
from jax.experimental.pallas import tpu as pltpu
from jax.sharding import PartitionSpec as P

HEADS = 16
HEAD_DIM = 64
WINDOW = 512
BLOCK = 64
DOCS = 4
PAIR = 2 * HEAD_DIM
MASKED = -1e30
BF16 = jnp.bfloat16
F32 = jnp.float32

VMEM = pl.BlockSpec(memory_space=pltpu.VMEM)
HBM = pl.BlockSpec(memory_space=pltpu.HBM)
ANY = pl.BlockSpec(memory_space=pl.ANY)
SMEM = pl.BlockSpec(memory_space=pltpu.SMEM)


def call(kernel, out_shape, operands, hbm=0, after=(), scratch=(), flops=0, moved=0, vmem=24):
    outs = [jax.ShapeDtypeStruct(shape, kind) for shape, kind in out_shape]
    operands = [
        pltpu.with_memory_space_constraint(value, pltpu.HBM) if i < hbm else value
        for i, value in enumerate(operands)
    ]
    count = len(operands)

    def run(*refs):
        kernel(*refs[:count], *refs[count + len(after) :])

    return pl.pallas_call(
        run,
        out_shape=outs,
        in_specs=[HBM] * hbm + [VMEM] * (count - hbm) + [ANY] * len(after),
        out_specs=[VMEM] * len(outs),
        scratch_shapes=list(scratch),
        compiler_params=pltpu.CompilerParams(vmem_limit_bytes=vmem << 20),
        cost_estimate=pl.CostEstimate(flops=flops, bytes_accessed=moved, transcendentals=0),
    )(*operands, *after)


def dot_nn(a, b):
    return lax.dot_general(a, b, (((1,), (0,)), ((), ())), preferred_element_type=F32)


def dot_nt(a, b):
    return lax.dot_general(a, b, (((1,), (1,)), ((), ())), preferred_element_type=F32)


def doc_bounds(len_ref):
    ends = []
    total = 0
    for d in range(DOCS):
        total = total + len_ref[0, d] * BLOCK
        ends.append(total)
    return ends


def query_limits(len_ref, first, count):
    ends = doc_bounds(len_ref)
    query = first + lax.broadcasted_iota(jnp.int32, (1, count), 1)
    low = jnp.zeros((1, count), jnp.int32)
    high = jnp.full((1, count), ends[DOCS - 1], jnp.int32)
    for d in range(DOCS - 1):
        low = jnp.where(query >= ends[d], ends[d], low)
        high = jnp.where(query < ends[DOCS - 2 - d], ends[DOCS - 2 - d], high)
    return jnp.maximum(low, query - WINDOW), jnp.minimum(high, query + WINDOW + 1)


def pack_kernel(group, fast, len_hbm, up_hbm, k_hbm, v_hbm, q_hbm, cot_hbm, weight_hbm, *refs):
    own_kv, far_kv, own_rest, near_all, far_rest = (
        refs[0], refs[1 : group - 1], refs[group - 1], refs[group], refs[group + 1 : 2 * group - 1]
    )
    limits = refs[2 * group - 1]
    k_ref, v_ref, q_ref, cot_ref, len_ref, up_ref, sems = refs[-7:]
    copies = [(len_hbm, len_ref), (up_hbm, up_ref), (k_hbm, k_ref), (v_hbm, v_ref)]
    copies += [(q_hbm, q_ref), (cot_hbm, cot_ref)]
    rows = q_ref.shape[0]
    cols = q_ref.shape[1] // group
    place = lax.axis_index("seq")
    inner = lax.rem(place, group)
    if fast:
        start = pl.multiple_of(lax.rem(inner, 2) * cols, 128)
        copies += [(weight_hbm.at[pl.ds(start, cols)], refs[2 * group])]
    loads = [
        pltpu.make_async_copy(source, target, sems.at[i])
        for i, (source, target) in enumerate(copies)
    ]
    for load in loads:
        load.start()
    starts = [pl.multiple_of((inner ^ m) * cols, 128) for m in range(group)]
    loads[2].wait()
    loads[3].wait()
    for m, target in ((0, own_kv), (1, near_all), *((m, far_kv[m - 2]) for m in range(2, group))):
        target[0:rows, :] = k_ref[:, pl.ds(starts[m], cols)]
        target[rows : 2 * rows, :] = v_ref[:, pl.ds(starts[m], cols)]
    loads[0].wait()
    loads[1].wait()
    ends = doc_bounds(len_ref)
    low, high = query_limits(len_ref, (place - inner) * rows, group * rows)
    limits[0:1, :] = low
    limits[1:2, :] = high
    pos = place * rows + lax.broadcasted_iota(jnp.int32, (rows, 1), 0)
    factor = jnp.full((rows, 1), up_ref[0, 0], jnp.int32)
    for d in range(1, DOCS):
        factor = jnp.where(pos >= ends[d - 1], up_ref[0, d], factor)
    loads[4].wait()
    own_rest[0:rows, :] = q_ref[:, pl.ds(starts[0], cols)]
    near_all[2 * rows : 3 * rows, :] = q_ref[:, pl.ds(starts[1], cols)]
    for m in range(2, group):
        far_rest[m - 2][0:rows, :] = q_ref[:, pl.ds(starts[m], cols)]
    loads[5].wait()
    weighted = (factor.astype(F32) * cot_ref[...].astype(F32)).astype(BF16)
    for j in range(group):
        part = weighted[:, j * cols : (j + 1) * cols]
        own_rest[(j + 1) * rows : (j + 2) * rows, :] = part
        near_all[(j + 3) * rows : (j + 4) * rows, :] = part
        far_rest[0][(j + 1) * rows : (j + 2) * rows, :] = part
    if fast:
        loads[6].wait()


def join_kernel(*refs):
    out = refs[-1]
    size = out.shape[0] // (len(refs) - 1)
    for m, source in enumerate(refs[:-1]):
        out[m * size : (m + 1) * size, :] = source[0:size, :]


def pass_kernel(*refs):
    half = len(refs) // 2
    for source, target in zip(refs[:half], refs[half:]):
        target[...] = source[...]


def key_bias(limits, plane_start, block, rows, span):
    at = slice(block * rows, (block + 1) * rows)
    first = plane_start + (block * rows - WINDOW)
    key = first + lax.broadcasted_iota(jnp.int32, (span, rows), 0)
    seen = (key >= limits[0:1, at]) & (key < limits[1:2, at])
    bias = jnp.where(seen, 0.0, MASKED).astype(F32)
    return jnp.concatenate([bias, bias], axis=1)


def stack_pair(block):
    lane = lax.broadcasted_iota(jnp.int32, block.shape, 1)
    zero = jnp.zeros_like(block)
    return jnp.concatenate(
        [jnp.where(lane < HEAD_DIM, block, zero), jnp.where(lane < HEAD_DIM, zero, block)], axis=0
    )


def unstack_pair(both, rows):
    return jnp.concatenate([both[:HEAD_DIM, :rows], both[HEAD_DIM:, rows:]], axis=0)


def unit_slices(unit, pairs, rows, span):
    block, pair = unit // pairs, unit % pairs
    return (
        slice(block * rows, (block + 1) * rows),
        slice(block * rows, block * rows + span),
        slice(pair * PAIR, (pair + 1) * PAIR),
    )


LOG2_SCALE = math.log2(math.e) * HEAD_DIM ** (-0.5)


def forward_kernel(group, limits, *refs):
    own_kv, near_all = refs[0], refs[1]
    far_kv = refs[2:group]
    own_rest = refs[group]
    far_rest = refs[group + 1 : 2 * group - 1]
    sides = refs[2 * group - 1 : 2 * group + 3]
    keys, vals, keys_t, queries, att_t, att, stats, att_far, vals_t = refs[2 * group + 3 :]
    rows, cols = far_rest[-1].shape
    plane = group * rows
    span = rows + 2 * WINDOW
    place = lax.axis_index("seq")
    inner = lax.rem(place, group)
    plane_start = (place - inner) * rows
    even = 1 - lax.rem(place // group, 2)
    for m in range(group):
        spot = (inner ^ m) * rows
        asked = (own_rest, 0) if m == 0 else (near_all, 2 * rows) if m == 1 else (far_rest[m - 2], 0)
        at = pl.ds(pl.multiple_of(spot, 128), rows)
        queries[at, :] = asked[0][asked[1] : asked[1] + rows, :]
        held = own_kv if m == 0 else near_all if m == 1 else far_kv[m - 2]
        first, second = sides[0:2] if m == 0 else sides[2:4]
        base = max(m - 1, 0) * 2 * rows
        sources = [(held, 0, 1), (first, base, 2 * even), (second, base, 2 - 2 * even)]
        for source, base, side in sources:
            at = pl.ds(pl.multiple_of(side * plane + spot, 128), rows)
            keys[at, :] = source[base : base + rows, :]
            vals[at, :] = source[base + rows : base + 2 * rows, :]
    keys_t[...] = keys[...].T
    vals_t[...] = vals[...].T
    pairs = cols // PAIR
    count = group * pairs

    def scored(unit, bias):
        at, seen, lanes = unit_slices(unit, pairs, rows, span)
        return dot_nt(keys[seen, lanes], stack_pair(queries[at, lanes])) + bias

    def mix(unit, prob):
        at, seen, lanes = unit_slices(unit, pairs, rows, span)
        mixed = unstack_pair(dot_nn(vals_t[lanes, seen], prob), rows).astype(BF16)
        att_t[lanes, at] = mixed
        att[at, lanes] = mixed.T

    bias = key_bias(limits, plane_start, 0, rows, span)
    ahead = scored(0, bias)
    prob = None
    for unit in range(count):
        score = ahead
        if unit + 1 < count:
            if (unit + 1) % pairs == 0:
                bias = key_bias(limits, plane_start, (unit + 1) // pairs, rows, span)
            ahead = scored(unit + 1, bias)
        if unit > 0:
            mix(unit - 1, prob)
        peak = jnp.max(score, axis=0, keepdims=True)
        power = jnp.exp2((score - peak) * LOG2_SCALE)
        share = 1.0 / jnp.sum(power, axis=0, keepdims=True)
        stats[unit, 0:1, :] = peak
        stats[unit, 1:2, :] = share
        prob = (power * share).astype(BF16)
    mix(count - 1, prob)
    for m in range(2, group):
        taken = pl.ds(pl.multiple_of((inner ^ m) * rows, 128), rows)
        att_far[(m - 2) * rows : (m - 1) * rows, :] = att[taken, :]


def middle_kernel(group, fast, att_t, near, far, *refs):
    grads = refs[:group]
    grad_att = refs[group]
    out = refs[group + 1 : -3]
    grad_all, weight, total = refs[-3:]
    rows = grad_all.shape[0] // group
    cols = att_t.shape[0]
    place = lax.axis_index("seq")
    inner = lax.rem(place, group)
    if fast:
        is_near = inner // 2 == lax.axis_index("doc")

        @pl.when(is_near)
        def _():
            weight[...] = near[...]

        @pl.when(jnp.logical_not(is_near))
        def _():
            weight[...] = far[...]

    else:
        weight[...] = near[...]
    for m in range(group):
        skipped = grads[m].shape[0] - group * rows
        for j in range(group):
            grad_all[
                pl.ds(pl.multiple_of((inner ^ m) * rows, 128), rows), j * cols : (j + 1) * cols
            ] = grads[m][skipped + j * rows : skipped + (j + 1) * rows, :]
    product = dot_nn(att_t[...], grad_all[...])
    if fast:
        total[...] = product.astype(BF16)
        count = len(out)
        part = cols // count
        outer = place // group
        for m in range(count):
            out[m][...] = total[pl.ds(pl.multiple_of((outer ^ m) * part, 16), part), :]
    else:
        out[0][...] = product
    grad_att[...] = dot_nt(grad_all[...], weight[...]).astype(BF16)


def backward_kernel(
    group, limits, keys, vals, keys_t, queries, grad_att, stats,
    to_first, own, to_second, *refs,
):
    mine, near, far, key_sum, value_sum, grad_query = refs
    plane, cols = queries.shape
    rows = plane // group
    span = rows + 2 * WINDOW
    pairs = cols // PAIR
    count = group * pairs
    place = lax.axis_index("seq")
    inner = lax.rem(place, group)
    plane_start = (place - inner) * rows
    key_sum[...] = jnp.zeros_like(key_sum)
    value_sum[...] = jnp.zeros_like(value_sum)

    def begin(unit, bias):
        at, seen, lanes = unit_slices(unit, pairs, rows, span)
        query = stack_pair(queries[at, lanes])
        grad = stack_pair(grad_att[at, lanes])
        score = dot_nt(keys[seen, lanes], query) + bias
        return query, grad, score, dot_nt(vals[seen, lanes], grad)

    def end(unit, query, grad, prob, grad_score):
        at, seen, lanes = unit_slices(unit, pairs, rows, span)
        value_sum[seen, lanes] += dot_nn(prob, grad)
        key_sum[seen, lanes] += dot_nn(grad_score, query)
        turned = unstack_pair(dot_nn(keys_t[lanes, seen], grad_score), rows)
        grad_query[at, lanes] = turned.astype(BF16).T

    bias = key_bias(limits, plane_start, 0, rows, span)
    ahead = begin(0, bias)
    behind = None
    for unit in range(count):
        query, grad, score, grad_prob = ahead
        if unit + 1 < count:
            if (unit + 1) % pairs == 0:
                bias = key_bias(limits, plane_start, (unit + 1) // pairs, rows, span)
            ahead = begin(unit + 1, bias)
        if unit > 0:
            end(unit - 1, *behind)
        prob = jnp.exp2((score - stats[unit, 0:1, :]) * LOG2_SCALE) * stats[unit, 1:2, :]
        centre = jnp.sum(prob * grad_prob, axis=0, keepdims=True)
        grad_score = (prob * (grad_prob - centre) * HEAD_DIM ** (-0.5)).astype(BF16)
        behind = (query, grad, prob.astype(BF16), grad_score)
    end(count - 1, *behind)
    for m, (target, base) in enumerate(((mine, 0), (near, 0), (far, 0), (far, rows))):
        taken = pl.ds(pl.multiple_of((inner ^ m) * rows, 128), rows)
        target[base : base + rows, :] = grad_query[taken, :]
    even = 1 - lax.rem(place // group, 2)
    for target, side in ((to_first, 2 * even), (own, 1), (to_second, 2 - 2 * even)):
        kept = pl.ds(pl.multiple_of(side * plane, 128), plane)
        target[0:plane, :] = key_sum[kept, :].astype(target.dtype)
        target[plane : 2 * plane, :] = value_sum[kept, :].astype(target.dtype)


def settle_kernel(group, own, from_first, from_second, *pieces):
    rows = pieces[0].shape[0] // 2
    plane = group * rows
    inner = lax.rem(lax.axis_index("seq"), group)
    for m in range(group):
        spot = (inner ^ m) * rows
        for part in range(2):
            at = pl.ds(pl.multiple_of(part * plane + spot, 128), rows)
            summed = own[at, :] + from_first[at, :].astype(F32) + from_second[at, :].astype(F32)
            pieces[m][part * rows : (part + 1) * rows, :] = summed.astype(BF16)


def relay_kernel(group, near, far, att, att_far, out):
    rows = near.shape[0]
    inner = lax.rem(lax.axis_index("seq"), group)
    out[0:rows, :] = near[...]
    out[rows : 2 * rows, :] = far[rows : 2 * rows, :]
    out[2 * rows : 3 * rows, :] = att[pl.ds(pl.multiple_of((inner ^ 1) * rows, 128), rows), :]
    out[3 * rows : 4 * rows, :] = att_far[rows : 2 * rows, :]


def unpack_kernel(group, *refs):
    pieces, outs = refs[:group], refs[group:]
    rows, width = outs[0].shape
    cols = width // group
    inner = lax.rem(lax.axis_index("seq"), group)
    for m in range(group):
        at = pl.ds(pl.multiple_of((inner ^ m) * cols, 128), cols)
        for part in range(2):
            outs[part][:, at] = pieces[m][part * rows : (part + 1) * rows, :]


def project_kernel(
    group, fast, near, far, farther, mine, early, att_mine, att_early, relayed,
    grad_query, out, done, att,
):
    rows, width = out.shape
    cols = width // group
    half = width // 2
    inner = lax.rem(lax.axis_index("seq"), group)
    first = lax.axis_index("doc") if fast else 0
    own = pl.ds(pl.multiple_of(inner * rows, 128), rows)
    held = (
        (mine[...], att_mine[own, :]),
        (relayed[0:rows, :], relayed[2 * rows : 3 * rows, :]),
        (early[0:rows, :], att_early[0:rows, :]),
        (relayed[rows : 2 * rows, :], relayed[3 * rows : 4 * rows, :]),
    )
    for m in range(group):
        at = pl.ds(pl.multiple_of((inner ^ m) * cols, 128), cols)
        grad_query[:, at], att[:, at] = held[m]
    total = dot_nn(att[:, pl.ds(pl.multiple_of(first * half, 128), half)], near[...])
    for side, weight in ((0, far), (1, farther)):
        start = (1 - first) * half + (lax.rem(inner, 2) ^ side) * cols
        total += dot_nn(att[:, pl.ds(pl.multiple_of(start, 128), cols)], weight[...])
    out[...] = total.astype(BF16)
    done[...] = jnp.zeros_like(done)


def add_kernel(*refs):
    total = refs[0][...].astype(F32)
    for ref in refs[1:-1]:
        total += ref[...].astype(F32)
    refs[-1][...] = total.astype(BF16)


def cross_kernel(group, own, first, second, out):
    inner = lax.rem(lax.axis_index("seq"), group)
    owner = inner // 2 == lax.axis_index("doc")

    @pl.when(owner)
    def _():
        out[...] = (first[...].astype(F32) + own[...].astype(F32)).astype(BF16)

    @pl.when(jnp.logical_not(owner))
    def _():
        out[...] = (first[...].astype(F32) + second[...].astype(F32)).astype(BF16)


def gather_kernel(group, *refs):
    out = refs[-1]
    outer = lax.axis_index("seq") // group
    part = refs[0].shape[0]
    for m, source in enumerate(refs[:-1]):
        out[pl.ds(pl.multiple_of((outer ^ m) * part, 16), part), :] = source[...]


def finish_kernel(scale, near, far, out):
    side = lax.rem(lax.axis_index("seq"), 2)
    size = near.shape[0]
    for source, base in ((near, side), (far, 1 - side)):
        at = pl.ds(pl.multiple_of(base * size, 128), size)
        out[at, :] = source[...].astype(F32) * scale


def body(queries, key_rows, value_rows, cotangent, out_weight, lengths, upweight):
    rows = queries.shape[1]
    width = queries.shape[2]
    seq_count = lax.axis_size("seq")
    doc_count = lax.axis_size("doc")
    group = WINDOW // rows
    plane = group * rows
    cols = width // group
    pairs = cols // PAIR
    outer_count = seq_count // group
    units = group * pairs
    span = rows + 2 * WINDOW
    fast = doc_count == 2 and outer_count == 4
    scale = 1.0 / math.sqrt(rows * seq_count * doc_count)

    def inner_swap(value, m):
        return lax.ppermute(value, "seq", [(i, i ^ m) for i in range(seq_count)])

    def outer_swap(value, m):
        return lax.ppermute(value, "seq", [(i, i ^ (m * group)) for i in range(seq_count)])

    def outer_first(value):
        return outer_swap(value, 1)

    def outer_second(value):
        pairs_of = [(i, (((i // group + 1) ^ 1) - 1) * group + i % group) for i in range(seq_count)]
        return lax.ppermute(value, "seq", [(a, b) for a, b in pairs_of if 0 <= b < seq_count])

    tokens = (rows, width)
    rest = [(((1 + group) * rows, cols), BF16), ((rows, cols), BF16)]
    chunk = [((cols, width), BF16)] if fast else []
    own_kv, *packed = call(
        functools.partial(pack_kernel, group, fast),
        [((2 * rows, cols), BF16)] * (group - 1)
        + [rest[0], (((3 + group) * rows, cols), BF16), *rest]
        + [((8, plane), jnp.int32), *chunk],
        (lengths, upweight, key_rows[0], value_rows[0], queries[0], cotangent[0], out_weight),
        hbm=7,
        scratch=[pltpu.VMEM(tokens, BF16)] * 4
        + [pltpu.SMEM((1, DOCS), jnp.int32)] * 2
        + [pltpu.SemaphoreType.DMA((7,))],
        flops=1 << 20, moved=4 << 20,
    )
    far_kv = [inner_swap(packed[m - 2], m) for m in range(2, group)]
    own_rest, near_all, rest_first, rest_last, limits, *weight = packed[group - 2 :]
    near_all = inner_swap(near_all, 1)
    (sent_kv,) = call(
        pass_kernel, [((2 * rows, cols), BF16)], (own_kv,), flops=3 << 30, moved=1 << 18
    )
    sides = [outer_first(sent_kv), outer_second(sent_kv)]
    rest_first, rest_last = call(
        pass_kernel, rest, (rest_first, rest_last),
        after=(near_all, *far_kv), flops=1 << 18, moved=1 << 20,
    )
    far_rest = [inner_swap(rest_first, 2), inner_swap(rest_last, 3)]
    (joined,) = call(
        join_kernel, [((2 * (group - 1) * rows, cols), BF16)], (near_all, *far_kv),
        after=(rest_last, *sides), flops=3 << 30, moved=1 << 20,
    )
    sides += [outer_first(joined), outer_second(joined)]
    grads = [own_rest, near_all, far_rest[0], inner_swap(far_rest[0], 1)]
    inner = lax.axis_index("seq") % group
    if fast:
        near, half_near = weight[0], out_weight
        far = lax.ppermute(near, "doc", [(0, 1), (1, 0)])
        half_far = [far, inner_swap(far, 1)]
    else:
        whole = lax.all_gather(out_weight, "doc", axis=0, tiled=True)
        chunks = [lax.dynamic_slice_in_dim(whole, at * cols, cols, 0) for at in (
            inner, 2 + inner % 2, 2 + (inner + 1) % 2
        )]
        near = far = chunks[0]
        half_near, half_far = whole[: width // 2], chunks[1:]

    keys, vals, keys_t, query_all, att_t, att, stats, att_far = call(
        functools.partial(forward_kernel, group),
        [((3 * plane, cols), BF16)] * 2
        + [((cols, 3 * plane), BF16), ((plane, cols), BF16), ((cols, plane), BF16)]
        + [((plane, cols), BF16), ((units, 8, 2 * rows), F32), ((2 * rows, cols), BF16)],
        (limits, own_kv, near_all, *far_kv, own_rest, *far_rest, *sides),
        scratch=[pltpu.VMEM((cols, 3 * plane), BF16)],
        flops=4 << 30, moved=4 << 20, vmem=32,
    )
    att_early = inner_swap(att_far, 2)
    middle_out = (
        [((cols // outer_count, width), BF16)] * outer_count if fast else [((cols, width), F32)]
    )
    grad_att, *weight_parts = call(
        functools.partial(middle_kernel, group, fast),
        [((plane, cols), BF16)] + middle_out,
        (att_t, near, far, *grads),
        scratch=[
            pltpu.VMEM((plane, width), BF16),
            pltpu.VMEM((cols, width), BF16),
            pltpu.VMEM((cols, width), BF16),
        ],
        flops=1 << 30, moved=4 << 20,
    )

    to_first, own, to_second, early_own, early_near, early_far = call(
        functools.partial(backward_kernel, group),
        [((2 * plane, cols), BF16), ((2 * plane, cols), F32), ((2 * plane, cols), BF16)]
        + [((rows, cols), BF16)] * 2
        + [((2 * rows, cols), BF16)],
        (limits, keys, vals, keys_t, query_all, grad_att, stats),
        after=half_far[1:],
        scratch=[pltpu.VMEM((3 * plane, cols), F32)] * 2 + [pltpu.VMEM((plane, cols), BF16)],
        flops=8 << 30, moved=4 << 20, vmem=32,
    )
    if fast:
        swapped = [weight_parts[0]] + [outer_swap(weight_parts[m], m) for m in range(1, outer_count)]
        part_shape = [(swapped[0].shape, BF16)]
        (line,) = call(
            add_kernel, part_shape, swapped, after=(early_near,), flops=1 << 18, moved=1 << 19
        )
        (early_far,) = call(
            pass_kernel, [(early_far.shape, BF16)], (early_far,), after=(swapped[1],),
            flops=2 << 30, moved=1 << 19,
        )
        flat = [(d, i) for d in range(doc_count) for i in range(seq_count)]
        first_pairs, second_pairs = [], []
        for d, i in flat:
            owner = (i % group) // 2
            source = d * seq_count + i
            if d == owner:
                first_pairs.append((source, d * seq_count + (i ^ 2)))
            else:
                first_pairs.append((source, owner * seq_count + i))
                second_pairs.append((source, owner * seq_count + (i ^ 2)))
        got_first = lax.ppermute(line, ("doc", "seq"), first_pairs)
        got_second = lax.ppermute(line, ("doc", "seq"), second_pairs)
        early = inner_swap(early_far, 2)
        (final,) = call(
            functools.partial(cross_kernel, group), part_shape, (line, got_first, got_second), after=(early,),
            flops=2 << 30, moved=1 << 19,
        )
        gathered = [final] + [outer_swap(final, m) for m in range(1, outer_count)]
        before_settle = gathered[:1]
    else:
        placed = lax.dynamic_update_slice_in_dim(
            jnp.zeros((width, width), F32), weight_parts[0], inner * cols, 0
        )
        block = lax.psum_scatter(placed, "doc", scatter_dimension=0, tiled=True)
        grad_weight = lax.psum(block, "seq") * scale
        before_settle = ()
        early = inner_swap(early_far, 2)

    (relayed,) = call(
        functools.partial(relay_kernel, group), [((4 * rows, cols), BF16)],
        (early_near, early, att, att_early),
        after=(), flops=1 << 18, moved=1 << 20,
    )
    relayed = inner_swap(relayed, 1)
    grad_query, layer_out, projected = call(
        functools.partial(project_kernel, group, fast),
        [((rows, width), BF16)] * 2 + [((8, 128), F32)],
        (half_near, *half_far, early_own, early, att, att_early, relayed),
        scratch=[pltpu.VMEM((rows, width), BF16)],
        flops=1 << 30, moved=4 << 20,
    )
    sums = call(
        functools.partial(settle_kernel, group),
        [((2 * rows, cols), BF16)] * group,
        (own, outer_first(to_first), outer_second(to_second)),
        after=before_settle, flops=10 << 30, moved=2 << 20,
    )
    sums = [sums[0]] + [inner_swap(sums[m], m) for m in range(1, group)]
    if fast:
        (gathered,) = call(
            functools.partial(gather_kernel, group), [((cols, width), BF16)], gathered,
            after=(*sums[1:], projected), flops=1 << 18, moved=1 << 20,
        )
        (grad_weight,) = call(
            functools.partial(finish_kernel, scale), [((width // doc_count, width), F32)],
            (gathered, inner_swap(gathered, 1)), flops=1 << 20, moved=4 << 20,
        )
    grad_key, grad_value = call(
        functools.partial(unpack_kernel, group), [((rows, width), BF16)] * 2, sums,
        flops=1 << 20, moved=1 << 20,
    )
    return (layer_out[None], grad_query[None], grad_key[None], grad_value[None], grad_weight)


def solution(mesh):
    spec = P("doc", "seq", None)
    return jax.shard_map(
        body,
        mesh=mesh,
        in_specs=(spec, spec, spec, spec, P("doc", None), P("doc", None), P("doc", None)),
        out_specs=(spec, spec, spec, spec, P("doc", None)),
        check_vma=False,
    )
```

```python
import functools
import math

import jax
import jax.numpy as jnp
from jax import lax
from jax.experimental import pallas as pl
from jax.experimental.pallas import tpu as pltpu
from jax.sharding import PartitionSpec as P

HEADS = 16
HEAD_DIM = 64
WINDOW = 512
BLOCK = 64
DOCS = 4
PAIR = 2 * HEAD_DIM
MASKED = -1e30
BF16 = jnp.bfloat16
F32 = jnp.float32

VMEM = pl.BlockSpec(memory_space=pltpu.VMEM)
HBM = pl.BlockSpec(memory_space=pltpu.HBM)
ANY = pl.BlockSpec(memory_space=pl.ANY)
SMEM = pl.BlockSpec(memory_space=pltpu.SMEM)


def call(kernel, out_shape, operands, hbm=0, after=(), scratch=(), flops=0, moved=0, vmem=24):
    outs = [jax.ShapeDtypeStruct(shape, kind) for shape, kind in out_shape]
    operands = [
        pltpu.with_memory_space_constraint(value, pltpu.HBM) if i < hbm else value
        for i, value in enumerate(operands)
    ]
    count = len(operands)

    def run(*refs):
        kernel(*refs[:count], *refs[count + len(after) :])

    return pl.pallas_call(
        run,
        out_shape=outs,
        in_specs=[HBM] * hbm + [VMEM] * (count - hbm) + [ANY] * len(after),
        out_specs=[VMEM] * len(outs),
        scratch_shapes=list(scratch),
        compiler_params=pltpu.CompilerParams(vmem_limit_bytes=vmem << 20),
        cost_estimate=pl.CostEstimate(flops=flops, bytes_accessed=moved, transcendentals=0),
    )(*operands, *after)


def dot_nn(a, b):
    return lax.dot_general(a, b, (((1,), (0,)), ((), ())), preferred_element_type=F32)


def dot_nt(a, b):
    return lax.dot_general(a, b, (((1,), (1,)), ((), ())), preferred_element_type=F32)


def doc_bounds(len_ref):
    ends = []
    total = 0
    for d in range(DOCS):
        total = total + len_ref[0, d] * BLOCK
        ends.append(total)
    return ends


def query_limits(len_ref, first, count):
    ends = doc_bounds(len_ref)
    query = first + lax.broadcasted_iota(jnp.int32, (1, count), 1)
    low = jnp.zeros((1, count), jnp.int32)
    high = jnp.full((1, count), ends[DOCS - 1], jnp.int32)
    for d in range(DOCS - 1):
        low = jnp.where(query >= ends[d], ends[d], low)
        high = jnp.where(query < ends[DOCS - 2 - d], ends[DOCS - 2 - d], high)
    return jnp.maximum(low, query - WINDOW), jnp.minimum(high, query + WINDOW + 1)


def pack_kernel(group, fast, len_hbm, up_hbm, k_hbm, v_hbm, q_hbm, cot_hbm, weight_hbm, *refs):
    own_kv, far_kv, own_rest, near_all, far_rest = (
        refs[0], refs[1 : group - 1], refs[group - 1], refs[group], refs[group + 1 : 2 * group - 1]
    )
    limits = refs[2 * group - 1]
    k_ref, v_ref, q_ref, cot_ref, len_ref, up_ref, sems = refs[-7:]
    copies = [(len_hbm, len_ref), (up_hbm, up_ref), (k_hbm, k_ref), (v_hbm, v_ref)]
    copies += [(q_hbm, q_ref), (cot_hbm, cot_ref)]
    rows = q_ref.shape[0]
    cols = q_ref.shape[1] // group
    place = lax.axis_index("seq")
    inner = lax.rem(place, group)
    if fast:
        start = pl.multiple_of(lax.rem(inner, 2) * cols, 128)
        copies += [(weight_hbm.at[pl.ds(start, cols)], refs[2 * group])]
    loads = [
        pltpu.make_async_copy(source, target, sems.at[i])
        for i, (source, target) in enumerate(copies)
    ]
    for load in loads:
        load.start()
    starts = [pl.multiple_of((inner ^ m) * cols, 128) for m in range(group)]
    loads[2].wait()
    loads[3].wait()
    for m, target in ((0, own_kv), (1, near_all), *((m, far_kv[m - 2]) for m in range(2, group))):
        target[0:rows, :] = k_ref[:, pl.ds(starts[m], cols)]
        target[rows : 2 * rows, :] = v_ref[:, pl.ds(starts[m], cols)]
    loads[0].wait()
    loads[1].wait()
    ends = doc_bounds(len_ref)
    low, high = query_limits(len_ref, (place - inner) * rows, group * rows)
    limits[0:1, :] = low
    limits[1:2, :] = high
    pos = place * rows + lax.broadcasted_iota(jnp.int32, (rows, 1), 0)
    factor = jnp.full((rows, 1), up_ref[0, 0], jnp.int32)
    for d in range(1, DOCS):
        factor = jnp.where(pos >= ends[d - 1], up_ref[0, d], factor)
    loads[4].wait()
    own_rest[0:rows, :] = q_ref[:, pl.ds(starts[0], cols)]
    near_all[2 * rows : 3 * rows, :] = q_ref[:, pl.ds(starts[1], cols)]
    for m in range(2, group):
        far_rest[m - 2][0:rows, :] = q_ref[:, pl.ds(starts[m], cols)]
    loads[5].wait()
    weighted = (factor.astype(F32) * cot_ref[...].astype(F32)).astype(BF16)
    for j in range(group):
        part = weighted[:, j * cols : (j + 1) * cols]
        own_rest[(j + 1) * rows : (j + 2) * rows, :] = part
        near_all[(j + 3) * rows : (j + 4) * rows, :] = part
        far_rest[0][(j + 1) * rows : (j + 2) * rows, :] = part
    if fast:
        loads[6].wait()


def join_kernel(*refs):
    out = refs[-1]
    size = out.shape[0] // (len(refs) - 1)
    for m, source in enumerate(refs[:-1]):
        out[m * size : (m + 1) * size, :] = source[0:size, :]


def pass_kernel(*refs):
    half = len(refs) // 2
    for source, target in zip(refs[:half], refs[half:]):
        target[...] = source[...]


def key_bias(limits, plane_start, block, rows, span):
    at = slice(block * rows, (block + 1) * rows)
    first = plane_start + (block * rows - WINDOW)
    key = first + lax.broadcasted_iota(jnp.int32, (span, rows), 0)
    seen = (key >= limits[0:1, at]) & (key < limits[1:2, at])
    bias = jnp.where(seen, 0.0, MASKED).astype(F32)
    return jnp.concatenate([bias, bias], axis=1)


def stack_pair(block):
    lane = lax.broadcasted_iota(jnp.int32, block.shape, 1)
    zero = jnp.zeros_like(block)
    return jnp.concatenate(
        [jnp.where(lane < HEAD_DIM, block, zero), jnp.where(lane < HEAD_DIM, zero, block)], axis=0
    )


def unstack_pair(both, rows):
    return jnp.concatenate([both[:HEAD_DIM, :rows], both[HEAD_DIM:, rows:]], axis=0)


def unit_slices(unit, pairs, rows, span):
    block, pair = unit // pairs, unit % pairs
    return (
        slice(block * rows, (block + 1) * rows),
        slice(block * rows, block * rows + span),
        slice(pair * PAIR, (pair + 1) * PAIR),
    )


LOG2_SCALE = math.log2(math.e) * HEAD_DIM ** (-0.5)


def forward_kernel(group, limits, *refs):
    own_kv, near_all = refs[0], refs[1]
    far_kv = refs[2:group]
    own_rest = refs[group]
    far_rest = refs[group + 1 : 2 * group - 1]
    sides = refs[2 * group - 1 : 2 * group + 3]
    keys, vals, keys_t, queries, att_t, att, stats, att_far, vals_t = refs[2 * group + 3 :]
    rows, cols = far_rest[-1].shape
    plane = group * rows
    span = rows + 2 * WINDOW
    place = lax.axis_index("seq")
    inner = lax.rem(place, group)
    plane_start = (place - inner) * rows
    even = 1 - lax.rem(place // group, 2)
    for m in range(group):
        spot = (inner ^ m) * rows
        asked = (own_rest, 0) if m == 0 else (near_all, 2 * rows) if m == 1 else (far_rest[m - 2], 0)
        at = pl.ds(pl.multiple_of(spot, 128), rows)
        queries[at, :] = asked[0][asked[1] : asked[1] + rows, :]
        held = own_kv if m == 0 else near_all if m == 1 else far_kv[m - 2]
        first, second = sides[0:2] if m == 0 else sides[2:4]
        base = max(m - 1, 0) * 2 * rows
        sources = [(held, 0, 1), (first, base, 2 * even), (second, base, 2 - 2 * even)]
        for source, base, side in sources:
            at = pl.ds(pl.multiple_of(side * plane + spot, 128), rows)
            keys[at, :] = source[base : base + rows, :]
            vals[at, :] = source[base + rows : base + 2 * rows, :]
    keys_t[...] = keys[...].T
    vals_t[...] = vals[...].T
    pairs = cols // PAIR
    count = group * pairs

    def scored(unit, bias):
        at, seen, lanes = unit_slices(unit, pairs, rows, span)
        return dot_nt(keys[seen, lanes], stack_pair(queries[at, lanes])) + bias

    def mix(unit, prob):
        at, seen, lanes = unit_slices(unit, pairs, rows, span)
        mixed = unstack_pair(dot_nn(vals_t[lanes, seen], prob), rows).astype(BF16)
        att_t[lanes, at] = mixed
        att[at, lanes] = mixed.T

    bias = key_bias(limits, plane_start, 0, rows, span)
    ahead = scored(0, bias)
    prob = None
    for unit in range(count):
        score = ahead
        if unit + 1 < count:
            if (unit + 1) % pairs == 0:
                bias = key_bias(limits, plane_start, (unit + 1) // pairs, rows, span)
            ahead = scored(unit + 1, bias)
        if unit > 0:
            mix(unit - 1, prob)
        peak = jnp.max(score, axis=0, keepdims=True)
        power = jnp.exp2((score - peak) * LOG2_SCALE)
        share = 1.0 / jnp.sum(power, axis=0, keepdims=True)
        stats[unit, 0:1, :] = peak
        stats[unit, 1:2, :] = share
        prob = (power * share).astype(BF16)
    mix(count - 1, prob)
    for m in range(2, group):
        taken = pl.ds(pl.multiple_of((inner ^ m) * rows, 128), rows)
        att_far[(m - 2) * rows : (m - 1) * rows, :] = att[taken, :]


def middle_kernel(group, fast, att_t, near, far, *refs):
    grads = refs[:group]
    grad_att = refs[group]
    out = refs[group + 1 : -3]
    grad_all, weight, total = refs[-3:]
    rows = grad_all.shape[0] // group
    cols = att_t.shape[0]
    place = lax.axis_index("seq")
    inner = lax.rem(place, group)
    if fast:
        is_near = inner // 2 == lax.axis_index("doc")

        @pl.when(is_near)
        def _():
            weight[...] = near[...]

        @pl.when(jnp.logical_not(is_near))
        def _():
            weight[...] = far[...]

    else:
        weight[...] = near[...]
    for m in range(group):
        skipped = grads[m].shape[0] - group * rows
        for j in range(group):
            grad_all[
                pl.ds(pl.multiple_of((inner ^ m) * rows, 128), rows), j * cols : (j + 1) * cols
            ] = grads[m][skipped + j * rows : skipped + (j + 1) * rows, :]
    product = dot_nn(att_t[...], grad_all[...])
    if fast:
        total[...] = product.astype(BF16)
        count = len(out)
        part = cols // count
        outer = place // group
        for m in range(count):
            out[m][...] = total[pl.ds(pl.multiple_of((outer ^ m) * part, 16), part), :]
    else:
        out[0][...] = product
    grad_att[...] = dot_nt(grad_all[...], weight[...]).astype(BF16)


def backward_kernel(
    group, limits, keys, vals, keys_t, queries, grad_att, stats,
    to_first, own, to_second, *refs,
):
    mine, near, far, key_sum, value_sum, grad_query = refs
    plane, cols = queries.shape
    rows = plane // group
    span = rows + 2 * WINDOW
    pairs = cols // PAIR
    count = group * pairs
    place = lax.axis_index("seq")
    inner = lax.rem(place, group)
    plane_start = (place - inner) * rows
    key_sum[...] = jnp.zeros_like(key_sum)
    value_sum[...] = jnp.zeros_like(value_sum)

    def begin(unit, bias):
        at, seen, lanes = unit_slices(unit, pairs, rows, span)
        query = stack_pair(queries[at, lanes])
        grad = stack_pair(grad_att[at, lanes])
        score = dot_nt(keys[seen, lanes], query) + bias
        return query, grad, score, dot_nt(vals[seen, lanes], grad)

    def end(unit, query, grad, prob, grad_score):
        at, seen, lanes = unit_slices(unit, pairs, rows, span)
        value_sum[seen, lanes] += dot_nn(prob, grad)
        key_sum[seen, lanes] += dot_nn(grad_score, query)
        turned = unstack_pair(dot_nn(keys_t[lanes, seen], grad_score), rows)
        grad_query[at, lanes] = turned.astype(BF16).T

    bias = key_bias(limits, plane_start, 0, rows, span)
    ahead = begin(0, bias)
    behind = None
    for unit in range(count):
        query, grad, score, grad_prob = ahead
        if unit + 1 < count:
            if (unit + 1) % pairs == 0:
                bias = key_bias(limits, plane_start, (unit + 1) // pairs, rows, span)
            ahead = begin(unit + 1, bias)
        if unit > 0:
            end(unit - 1, *behind)
        prob = jnp.exp2((score - stats[unit, 0:1, :]) * LOG2_SCALE) * stats[unit, 1:2, :]
        centre = jnp.sum(prob * grad_prob, axis=0, keepdims=True)
        grad_score = (prob * (grad_prob - centre) * HEAD_DIM ** (-0.5)).astype(BF16)
        behind = (query, grad, prob.astype(BF16), grad_score)
    end(count - 1, *behind)
    for m, (target, base) in enumerate(((mine, 0), (near, 0), (far, 0), (far, rows))):
        taken = pl.ds(pl.multiple_of((inner ^ m) * rows, 128), rows)
        target[base : base + rows, :] = grad_query[taken, :]
    even = 1 - lax.rem(place // group, 2)
    for target, side in ((to_first, 2 * even), (own, 1), (to_second, 2 - 2 * even)):
        kept = pl.ds(pl.multiple_of(side * plane, 128), plane)
        target[0:plane, :] = key_sum[kept, :].astype(target.dtype)
        target[plane : 2 * plane, :] = value_sum[kept, :].astype(target.dtype)


def settle_kernel(group, own, from_first, from_second, *pieces):
    rows = pieces[0].shape[0] // 2
    plane = group * rows
    inner = lax.rem(lax.axis_index("seq"), group)
    for m in range(group):
        spot = (inner ^ m) * rows
        for part in range(2):
            at = pl.ds(pl.multiple_of(part * plane + spot, 128), rows)
            summed = own[at, :] + from_first[at, :].astype(F32) + from_second[at, :].astype(F32)
            pieces[m][part * rows : (part + 1) * rows, :] = summed.astype(BF16)


def relay_kernel(group, near, far, att, att_far, out):
    rows = near.shape[0]
    inner = lax.rem(lax.axis_index("seq"), group)
    out[0:rows, :] = near[...]
    out[rows : 2 * rows, :] = far[rows : 2 * rows, :]
    out[2 * rows : 3 * rows, :] = att[pl.ds(pl.multiple_of((inner ^ 1) * rows, 128), rows), :]
    out[3 * rows : 4 * rows, :] = att_far[rows : 2 * rows, :]


def unpack_kernel(group, *refs):
    pieces, outs = refs[:group], refs[group:]
    rows, width = outs[0].shape
    cols = width // group
    inner = lax.rem(lax.axis_index("seq"), group)
    for m in range(group):
        at = pl.ds(pl.multiple_of((inner ^ m) * cols, 128), cols)
        for part in range(2):
            outs[part][:, at] = pieces[m][part * rows : (part + 1) * rows, :]


def project_kernel(
    group, fast, near, far, farther, mine, early, att_mine, att_early, relayed,
    grad_query, out, done, att,
):
    rows, width = out.shape
    cols = width // group
    half = width // 2
    inner = lax.rem(lax.axis_index("seq"), group)
    first = lax.axis_index("doc") if fast else 0
    own = pl.ds(pl.multiple_of(inner * rows, 128), rows)
    held = (
        (mine[...], att_mine[own, :]),
        (relayed[0:rows, :], relayed[2 * rows : 3 * rows, :]),
        (early[0:rows, :], att_early[0:rows, :]),
        (relayed[rows : 2 * rows, :], relayed[3 * rows : 4 * rows, :]),
    )
    for m in range(group):
        at = pl.ds(pl.multiple_of((inner ^ m) * cols, 128), cols)
        grad_query[:, at], att[:, at] = held[m]
    total = dot_nn(att[:, pl.ds(pl.multiple_of(first * half, 128), half)], near[...])
    for side, weight in ((0, far), (1, farther)):
        start = (1 - first) * half + (lax.rem(inner, 2) ^ side) * cols
        total += dot_nn(att[:, pl.ds(pl.multiple_of(start, 128), cols)], weight[...])
    out[...] = total.astype(BF16)
    done[...] = jnp.zeros_like(done)


def add_kernel(*refs):
    total = refs[0][...].astype(F32)
    for ref in refs[1:-1]:
        total += ref[...].astype(F32)
    refs[-1][...] = total.astype(BF16)


def cross_kernel(group, own, first, second, out):
    inner = lax.rem(lax.axis_index("seq"), group)
    owner = inner // 2 == lax.axis_index("doc")

    @pl.when(owner)
    def _():
        out[...] = (first[...].astype(F32) + own[...].astype(F32)).astype(BF16)

    @pl.when(jnp.logical_not(owner))
    def _():
        out[...] = (first[...].astype(F32) + second[...].astype(F32)).astype(BF16)


def gather_kernel(group, *refs):
    out = refs[-1]
    outer = lax.axis_index("seq") // group
    part = refs[0].shape[0]
    for m, source in enumerate(refs[:-1]):
        out[pl.ds(pl.multiple_of((outer ^ m) * part, 16), part), :] = source[...]


def finish_kernel(scale, near, far, out):
    side = lax.rem(lax.axis_index("seq"), 2)
    size = near.shape[0]
    for source, base in ((near, side), (far, 1 - side)):
        at = pl.ds(pl.multiple_of(base * size, 128), size)
        out[at, :] = source[...].astype(F32) * scale


def body(queries, key_rows, value_rows, cotangent, out_weight, lengths, upweight):
    rows = queries.shape[1]
    width = queries.shape[2]
    seq_count = lax.axis_size("seq")
    doc_count = lax.axis_size("doc")
    group = WINDOW // rows
    plane = group * rows
    cols = width // group
    pairs = cols // PAIR
    outer_count = seq_count // group
    units = group * pairs
    span = rows + 2 * WINDOW
    fast = doc_count == 2 and outer_count == 4
    scale = 1.0 / math.sqrt(rows * seq_count * doc_count)

    def inner_swap(value, m):
        return lax.ppermute(value, "seq", [(i, i ^ m) for i in range(seq_count)])

    def outer_swap(value, m):
        return lax.ppermute(value, "seq", [(i, i ^ (m * group)) for i in range(seq_count)])

    def outer_first(value):
        return outer_swap(value, 1)

    def outer_second(value):
        pairs_of = [(i, (((i // group + 1) ^ 1) - 1) * group + i % group) for i in range(seq_count)]
        return lax.ppermute(value, "seq", [(a, b) for a, b in pairs_of if 0 <= b < seq_count])

    tokens = (rows, width)
    rest = [(((1 + group) * rows, cols), BF16), ((rows, cols), BF16)]
    chunk = [((cols, width), BF16)] if fast else []
    own_kv, *packed = call(
        functools.partial(pack_kernel, group, fast),
        [((2 * rows, cols), BF16)] * (group - 1)
        + [rest[0], (((3 + group) * rows, cols), BF16), *rest]
        + [((8, plane), jnp.int32), *chunk],
        (lengths, upweight, key_rows[0], value_rows[0], queries[0], cotangent[0], out_weight),
        hbm=7,
        scratch=[pltpu.VMEM(tokens, BF16)] * 4
        + [pltpu.SMEM((1, DOCS), jnp.int32)] * 2
        + [pltpu.SemaphoreType.DMA((7,))],
        flops=1 << 20, moved=4 << 20,
    )
    far_kv = [inner_swap(packed[m - 2], m) for m in range(2, group)]
    own_rest, near_all, rest_first, rest_last, limits, *weight = packed[group - 2 :]
    near_all = inner_swap(near_all, 1)
    (sent_kv,) = call(
        pass_kernel, [((2 * rows, cols), BF16)], (own_kv,), flops=3 << 30, moved=1 << 18
    )
    sides = [outer_first(sent_kv), outer_second(sent_kv)]
    rest_first, rest_last = call(
        pass_kernel, rest, (rest_first, rest_last),
        after=(near_all, *far_kv), flops=1 << 18, moved=1 << 20,
    )
    far_rest = [inner_swap(rest_first, 2), inner_swap(rest_last, 3)]
    (joined,) = call(
        join_kernel, [((2 * (group - 1) * rows, cols), BF16)], (near_all, *far_kv),
        after=(rest_last, *sides), flops=3 << 30, moved=1 << 20,
    )
    sides += [outer_first(joined), outer_second(joined)]
    grads = [own_rest, near_all, far_rest[0], inner_swap(far_rest[0], 1)]
    inner = lax.axis_index("seq") % group
    if fast:
        near, half_near = weight[0], out_weight
        far = lax.ppermute(near, "doc", [(0, 1), (1, 0)])
        half_far = [far, inner_swap(far, 1)]
    else:
        whole = lax.all_gather(out_weight, "doc", axis=0, tiled=True)
        chunks = [lax.dynamic_slice_in_dim(whole, at * cols, cols, 0) for at in (
            inner, 2 + inner % 2, 2 + (inner + 1) % 2
        )]
        near = far = chunks[0]
        half_near, half_far = whole[: width // 2], chunks[1:]

    keys, vals, keys_t, query_all, att_t, att, stats, att_far = call(
        functools.partial(forward_kernel, group),
        [((3 * plane, cols), BF16)] * 2
        + [((cols, 3 * plane), BF16), ((plane, cols), BF16), ((cols, plane), BF16)]
        + [((plane, cols), BF16), ((units, 8, 2 * rows), F32), ((2 * rows, cols), BF16)],
        (limits, own_kv, near_all, *far_kv, own_rest, *far_rest, *sides),
        scratch=[pltpu.VMEM((cols, 3 * plane), BF16)],
        flops=4 << 30, moved=4 << 20, vmem=32,
    )
    att_early = inner_swap(att_far, 2)
    middle_out = (
        [((cols // outer_count, width), BF16)] * outer_count if fast else [((cols, width), F32)]
    )
    grad_att, *weight_parts = call(
        functools.partial(middle_kernel, group, fast),
        [((plane, cols), BF16)] + middle_out,
        (att_t, near, far, *grads),
        scratch=[
            pltpu.VMEM((plane, width), BF16),
            pltpu.VMEM((cols, width), BF16),
            pltpu.VMEM((cols, width), BF16),
        ],
        flops=1 << 30, moved=4 << 20,
    )

    to_first, own, to_second, early_own, early_near, early_far = call(
        functools.partial(backward_kernel, group),
        [((2 * plane, cols), BF16), ((2 * plane, cols), F32), ((2 * plane, cols), BF16)]
        + [((rows, cols), BF16)] * 2
        + [((2 * rows, cols), BF16)],
        (limits, keys, vals, keys_t, query_all, grad_att, stats),
        after=half_far[1:],
        scratch=[pltpu.VMEM((3 * plane, cols), F32)] * 2 + [pltpu.VMEM((plane, cols), BF16)],
        flops=8 << 30, moved=4 << 20, vmem=32,
    )
    if fast:
        swapped = [weight_parts[0]] + [outer_swap(weight_parts[m], m) for m in range(1, outer_count)]
        part_shape = [(swapped[0].shape, BF16)]
        (line,) = call(
            add_kernel, part_shape, swapped, after=(early_near,), flops=1 << 18, moved=1 << 19
        )
        (early_far,) = call(
            pass_kernel, [(early_far.shape, BF16)], (early_far,), after=(swapped[1],),
            flops=2 << 30, moved=1 << 19,
        )
        flat = [(d, i) for d in range(doc_count) for i in range(seq_count)]
        first_pairs, second_pairs = [], []
        for d, i in flat:
            owner = (i % group) // 2
            source = d * seq_count + i
            if d == owner:
                first_pairs.append((source, d * seq_count + (i ^ 2)))
            else:
                first_pairs.append((source, owner * seq_count + i))
                second_pairs.append((source, owner * seq_count + (i ^ 2)))
        got_first = lax.ppermute(line, ("doc", "seq"), first_pairs)
        got_second = lax.ppermute(line, ("doc", "seq"), second_pairs)
        early = inner_swap(early_far, 2)
        (final,) = call(
            functools.partial(cross_kernel, group), part_shape, (line, got_first, got_second),
            flops=2 << 30, moved=1 << 19,
        )
        gathered = [final] + [outer_swap(final, m) for m in range(1, outer_count)]
        before_settle = gathered[:1]
    else:
        placed = lax.dynamic_update_slice_in_dim(
            jnp.zeros((width, width), F32), weight_parts[0], inner * cols, 0
        )
        block = lax.psum_scatter(placed, "doc", scatter_dimension=0, tiled=True)
        grad_weight = lax.psum(block, "seq") * scale
        before_settle = ()
        early = inner_swap(early_far, 2)

    (relayed,) = call(
        functools.partial(relay_kernel, group), [((4 * rows, cols), BF16)],
        (early_near, early, att, att_early),
        after=(), flops=1 << 18, moved=1 << 20,
    )
    relayed = inner_swap(relayed, 1)
    grad_query, layer_out, projected = call(
        functools.partial(project_kernel, group, fast),
        [((rows, width), BF16)] * 2 + [((8, 128), F32)],
        (half_near, *half_far, early_own, early, att, att_early, relayed),
        scratch=[pltpu.VMEM((rows, width), BF16)],
        flops=1 << 30, moved=4 << 20,
    )
    sums = call(
        functools.partial(settle_kernel, group),
        [((2 * rows, cols), BF16)] * group,
        (own, outer_first(to_first), outer_second(to_second)),
        after=before_settle, flops=10 << 30, moved=2 << 20,
    )
    sums = [sums[0]] + [inner_swap(sums[m], m) for m in range(1, group)]
    if fast:
        (gathered,) = call(
            functools.partial(gather_kernel, group), [((cols, width), BF16)], gathered,
            after=(*sums[1:], projected), flops=1 << 18, moved=1 << 20,
        )
        (grad_weight,) = call(
            functools.partial(finish_kernel, scale), [((width // doc_count, width), F32)],
            (gathered, inner_swap(gathered, 1)), flops=1 << 20, moved=4 << 20,
        )
    grad_key, grad_value = call(
        functools.partial(unpack_kernel, group), [((rows, width), BF16)] * 2, sums,
        flops=1 << 20, moved=1 << 20,
    )
    return (layer_out[None], grad_query[None], grad_key[None], grad_value[None], grad_weight)


def solution(mesh):
    spec = P("doc", "seq", None)
    return jax.shard_map(
        body,
        mesh=mesh,
        in_specs=(spec, spec, spec, spec, P("doc", None), P("doc", None), P("doc", None)),
        out_specs=(spec, spec, spec, spec, P("doc", None)),
        check_vma=False,
    )
```
